128 devices in a mesh: rep: 4 (over y_lo, core), gx: 8 (over z, y_hi), gy: 4 (over x).
Axes of the slice: x: 4, y: 4 (y_hi: 2, y_lo: 2; y = y_hi * 2 + y_lo), z: 4, core: 2. Of those that a mesh axis runs over, the one named last changes fastest.
Arguments:
- node_feat: bfloat16 [32768, 256], P(('rep', 'gx', 'gy')), may hold values from -6 to 6
- edge_feat: bfloat16 [1048576, 256], P(('rep', 'gx', 'gy')), may hold values from -6 to 6
- edge_src: int32 [1048576], P(('rep', 'gx', 'gy')), may hold values from 0 to 1023
- edge_dst: int32 [1048576], P(('rep', 'gx', 'gy')), may hold values from 0 to 255
- edge_count: int32 [128], P(('rep', 'gx', 'gy')), may hold values from 2048 to 8192, as said below
- send_idx: int32 [4, 8, 4, 2, 2, 64], P('rep', 'gx', 'gy'), may hold values from 0 to 255
- w_qkv: bfloat16 [2, 256, 768], replicated, may hold values from -0.375 to 0.375
- w_edge: bfloat16 [2, 256, 256], replicated, may hold values from -0.375 to 0.375
- gains: float32 [2, 256], replicated, may hold values from 0.1 to 1.9
- head_in: bfloat16 [256, 256], replicated, may hold values from -0.375 to 0.375
- head_out: bfloat16 [256, 169], replicated, may hold values from -0.375 to 0.375
- targets: bfloat16 [169, 1048576], P(None, ('rep', 'gx', 'gy')), may hold values from -15 to 15
Outputs:
- node_out: bfloat16 [32768, 256], P(('rep', 'gx', 'gy'))
- grad_head_in: float32 [256, 256], replicated
- grad_head_out: float32 [256, 169], replicated
The draws below stay inside these ranges and needn't reach their ends.
Inputs may be any that keep to these rules, and one draw needn't show every extreme that they name: `edge_count`: edge slots of a tile at positions from its count on are padding; some tile holds 8192 live edges.
All inputs are finite; a program needn't handle non-finite values.
Results may differ from the reference program's by a relative error of at most 0.0025.
The reference program's roundings to bfloat16 on the way count: a program that leaves them out, or rounds other values in their place, can miss the bound.
Values may be sent and summed in bfloat16 or wider, within the bound.
No kernel may reach another device: no remote copies, remote signals or barrier semaphores. Data moves between devices by JAX's collectives and lax.ppermute only.
A program may use at most 128 MiB of HBM per device.

```python
import jax
import jax.numpy as jnp
from jax import lax

HIDDEN_SIZE = 256
ORB2 = 169
LAYERS = 2
GHOST_CELL = 64
ATOM_DEV = 256
EDGE_DEV = 8192
DEVS = 128
ATOMS = 32768
EDGES = 1048576
TABLE = 1024
N_REP = 4
N_GX = 8
N_GY = 4


def draw_edge_count(key, part):
    first_key, second_key = jax.random.split(jax.random.fold_in(key, 17))
    counts = jax.random.randint(first_key, (DEVS,), EDGE_DEV // 4, EDGE_DEV + 1)
    fullest = jax.random.randint(second_key, (), 0, DEVS)
    return jnp.where(jnp.arange(DEVS) == fullest, EDGE_DEV, counts).astype(jnp.int32)


def plant(array, own_key, low, largest):
    extent = array.shape
    index_at = [jax.random.randint(jax.random.fold_in(own_key, axis), (), 0, extent[axis]) for axis in range(len(extent))]
    array = array.at[tuple(index_at)].set(low)
    longest = extent.index(max(extent))
    index_at[longest] = (index_at[longest] + 1) % extent[longest]
    return array.at[tuple(index_at)].set(largest)


def block_scale(key, shape, cuts, low, largest):
    def one(position, shards_of):
        draws = jax.random.uniform(jax.random.fold_in(jax.random.fold_in(key, 6), position), (shards_of,), jnp.float32, low / len(cuts), largest / len(cuts))
        return jnp.repeat(jnp.exp(draws), shape[position] // shards_of).reshape((-1,) + (1,) * (len(shape) - position - 1))

    factor_of = one(*cuts[0])
    for cut in cuts[1:]:
        factor_of = factor_of * one(*cut)
    return factor_of


def centred(key, dims, deviation, reach, cuts=(), held_as=jnp.bfloat16):
    result = deviation * jax.random.normal(key, dims, jnp.float32)
    if cuts:
        result = result * block_scale(key, dims, cuts, -0.22, 0.18)
    return jnp.clip(result, -reach, reach).astype(held_as)


def setup_inputs(seed: int = 0) -> dict:
    streams_of = jax.random.split(jax.random.key(seed), 13)
    node_feat = centred(streams_of[0], (ATOMS, HIDDEN_SIZE), 1.0, 6.0, ((0, 128),))
    edge_feat = centred(streams_of[1], (EDGES, HIDDEN_SIZE), 1.0, 6.0, ((0, 128),))
    edge_src = plant(jax.random.randint(streams_of[2], (EDGES,), 0, TABLE), jax.random.fold_in(streams_of[2], 1), 0, TABLE - 1).astype(jnp.int32)
    edge_dst = plant(jax.random.randint(streams_of[3], (EDGES,), 0, ATOM_DEV), jax.random.fold_in(streams_of[3], 1), 0, ATOM_DEV - 1).astype(jnp.int32)
    edge_count = draw_edge_count(jax.random.fold_in(streams_of[12], 71), 0)
    send_idx = plant(jax.random.randint(streams_of[5], (N_REP, N_GX, N_GY, 2, 2, GHOST_CELL), 0, ATOM_DEV), jax.random.fold_in(streams_of[5], 1), 0, ATOM_DEV - 1).astype(jnp.int32)
    w_qkv = centred(streams_of[6], (LAYERS, HIDDEN_SIZE, 3 * HIDDEN_SIZE), HIDDEN_SIZE ** -0.5, 0.375)
    w_edge = centred(streams_of[7], (LAYERS, HIDDEN_SIZE, HIDDEN_SIZE), HIDDEN_SIZE ** -0.5, 0.375)
    gains = jnp.clip(1.0 + 0.18 * jax.random.normal(streams_of[8], (LAYERS, HIDDEN_SIZE), jnp.float32), 0.1, 1.9)
    head_in = centred(streams_of[9], (HIDDEN_SIZE, HIDDEN_SIZE), HIDDEN_SIZE ** -0.5, 0.375)
    head_out = centred(streams_of[10], (HIDDEN_SIZE, ORB2), HIDDEN_SIZE ** -0.5, 0.375)
    targets = centred(streams_of[11], (ORB2, EDGES), 2.5, 15.0, ((1, 128),))
    return {"node_feat": node_feat, "edge_feat": edge_feat, "edge_src": edge_src, "edge_dst": edge_dst, "edge_count": edge_count, "send_idx": send_idx, "w_qkv": w_qkv, "w_edge": w_edge, "gains": gains, "head_in": head_in, "head_out": head_out, "targets": targets}


OUTER_CELLS = ((0, 0), (0, 1), (0, 2), (0, 3), (1, 0), (1, 3), (2, 0), (2, 3), (3, 0), (3, 1), (3, 2), (3, 3))
CELL_SOURCE = ((-1, 1), (0, 0), (0, 1), (1, 0))

def layer_norm(values):
    centre = values - lax.optimization_barrier(jnp.mean(values, axis=-1, keepdims=True))
    spread = lax.optimization_barrier(jnp.mean(centre * centre, axis=-1, keepdims=True))
    return centre * lax.rsqrt(spread + 1e-05)

def build_ghosts(nodes, send_idx):
    flat_nodes = nodes.reshape(DEVS, ATOM_DEV, HIDDEN_SIZE)
    flat_index = send_idx.reshape(DEVS, 4 * GHOST_CELL).astype(jnp.int32)
    buffers = jax.vmap(lambda rows, picks: rows[picks])(flat_nodes, flat_index)
    buffers = buffers.reshape(N_REP, N_GX, N_GY, 2, 2, GHOST_CELL, HIDDEN_SIZE)
    slabs = []
    for cell_i, cell_j in OUTER_CELLS:
        offset_x, half_x = CELL_SOURCE[cell_i]
        offset_y, half_y = CELL_SOURCE[cell_j]
        slab = buffers[:, :, :, half_x, half_y]
        slab = jnp.roll(slab, shift=(-offset_x, -offset_y), axis=(1, 2))
        slabs.append(slab)
    ghosts = jnp.concatenate(slabs, axis=3)
    return ghosts.reshape(DEVS, 12 * GHOST_CELL, HIDDEN_SIZE)

def tile_layer(nodes, ghosts, edges, sources, receivers, live, weight_qkv, weight_edge, gain_row):
    projected = jnp.dot(nodes, weight_qkv, preferred_element_type=jnp.float32).astype(jnp.bfloat16)
    ghost_kv = jnp.dot(ghosts, weight_qkv[:, HIDDEN_SIZE:], preferred_element_type=jnp.float32).astype(jnp.bfloat16)
    table = jnp.concatenate([projected[:, HIDDEN_SIZE:], ghost_kv], axis=0)
    gathered = table[sources]
    queries = projected[:, :HIDDEN_SIZE][receivers]
    pre_act = queries.astype(jnp.float32) + gathered[:, :HIDDEN_SIZE].astype(jnp.float32)
    pre_act = pre_act + jnp.dot(edges, weight_edge, preferred_element_type=jnp.float32)
    new_edges = (edges.astype(jnp.float32) + live * jax.nn.silu(pre_act)).astype(jnp.bfloat16)
    weighted = live * jax.nn.sigmoid(pre_act) * gathered[:, HIDDEN_SIZE:].astype(jnp.float32)
    summed = jax.ops.segment_sum(weighted, receivers, num_segments=ATOM_DEV)
    new_nodes = (nodes.astype(jnp.float32) + gain_row * layer_norm(summed)).astype(jnp.bfloat16)
    return (new_nodes, new_edges)

def tile_readout(edges, live_row, target_block, head_in, head_out):
    scale = 0.125 / (EDGE_DEV * DEVS) ** 0.5
    act_in = jnp.dot(edges, head_in, preferred_element_type=jnp.float32)
    hidden_head = jax.nn.silu(act_in).astype(jnp.bfloat16)
    pred = lax.dot_general(head_out, hidden_head, (((0,), (1,)), ((), ())), preferred_element_type=jnp.float32)
    dpred = (live_row * (pred - target_block.astype(jnp.float32)) * scale).astype(jnp.bfloat16)
    dhidden = lax.dot_general(dpred, head_out, (((0,), (1,)), ((), ())), preferred_element_type=jnp.float32)
    sig = jax.nn.sigmoid(act_in)
    dact = (dhidden * sig * (1.0 + act_in * (1.0 - sig))).astype(jnp.bfloat16)
    grad_in = lax.dot_general(edges, dact, (((0,), (0,)), ((), ())), preferred_element_type=jnp.float32)
    grad_out = lax.dot_general(hidden_head, dpred, (((0,), (1,)), ((), ())), preferred_element_type=jnp.float32)
    return (grad_in, grad_out)

def reference(node_feat, edge_feat, edge_src, edge_dst, edge_count, send_idx, w_qkv, w_edge, gains, head_in, head_out, targets):
    nodes = node_feat.reshape(DEVS, ATOM_DEV, HIDDEN_SIZE)
    edges = edge_feat.reshape(DEVS, EDGE_DEV, HIDDEN_SIZE)
    sources = edge_src.reshape(DEVS, EDGE_DEV).astype(jnp.int32)
    receivers = edge_dst.reshape(DEVS, EDGE_DEV).astype(jnp.int32)
    positions = jnp.arange(EDGE_DEV, dtype=jnp.int32)
    live = (positions[None, :] < edge_count[:, None]).astype(jnp.float32)[:, :, None]
    for layer_index in range(LAYERS):
        ghosts = build_ghosts(nodes, send_idx)
        weight_qkv = w_qkv[layer_index]
        weight_edge = w_edge[layer_index]
        gain_row = gains[layer_index]

        def one_tile(items):
            return tile_layer(items[0], items[1], items[2], items[3], items[4], items[5], weight_qkv, weight_edge, gain_row)
        nodes, edges = lax.map(one_tile, (nodes, ghosts, edges, sources, receivers, live))
    target_tiles = jnp.transpose(targets.reshape(ORB2, DEVS, EDGE_DEV), (1, 0, 2))
    live_rows = live[:, :, 0][:, None, :]

    def readout(items):
        return tile_readout(items[0], items[1], items[2], head_in, head_out)
    grad_in, grad_out = lax.map(readout, (edges, live_rows, target_tiles))
    return (nodes.reshape(ATOMS, HIDDEN_SIZE), lax.optimization_barrier(jnp.sum(grad_in, axis=0)), lax.optimization_barrier(jnp.sum(grad_out, axis=0)))
```

```python
import functools

import jax
import jax.numpy as jnp
from jax import lax
from jax.experimental import pallas as pl
from jax.experimental.pallas import tpu as pltpu
from jax.sharding import PartitionSpec as P

AXES = ("rep", "gx", "gy")
BF = jnp.bfloat16
F32 = jnp.float32
BLOCK = 2048
SUB = 512


def nn(a, b):
    return jnp.dot(a, b, preferred_element_type=F32)


def nt(a, b):
    return lax.dot_general(a, b, (((1,), (1,)), ((), ())), preferred_element_type=F32)


def tn(a, b):
    return lax.dot_general(a, b, (((0,), (0,)), ((), ())), preferred_element_type=F32)


def hot(row, base, rows):
    index = lax.broadcasted_iota(jnp.int16, (rows, row.shape[1]), 0)
    same = index == (row - base).astype(jnp.int16)
    return jnp.where(same, jnp.ones((), BF), jnp.zeros((), BF))


def sigmoid(x):
    return 0.5 * jnp.tanh(0.5 * x) + 0.5


def pick_corners(nodes, index_row, c0_ref, c1_ref):
    rows = tn(hot(index_row, 0, 256), nodes).astype(BF)
    for j in range(2):
        c0_ref[j] = rows[64 * j : 64 * j + 64]
        c1_ref[j] = rows[128 + 64 * j : 192 + 64 * j]


def corner_kernel(nodes_ref, index_ref, c0_ref, c1_ref):
    pick_corners(nodes_ref[...], index_ref[...], c0_ref, c1_ref)


def prepare(nodes_ref, before_ref, after_ref, low_ref, high_ref, wqkv_ref, wedge_ref, node_t, wkv_t, wqe_t):
    nodes = nodes_ref[...]
    cells = (
        low_ref[0], before_ref[0], before_ref[1], high_ref[0],
        low_ref[1], high_ref[1], low_ref[2], high_ref[2],
        low_ref[3], after_ref[0], after_ref[1], high_ref[3],
    )
    node_t[:, 0:256] = nodes.T
    for k in range(3):
        node_t[:, 256 * (k + 1) : 256 * (k + 2)] = jnp.concatenate(cells[4 * k : 4 * k + 4], axis=0).T
    wkv_t[...] = wqkv_ref[:, 256:].T
    wqe_t[:, 0:256] = nn(nodes, wqkv_ref[:, 0:256]).astype(BF).T
    wqe_t[:, 256:512] = wedge_ref[...].T


def edge_part(edges_t, source, target, node_t, wkv_t, wqe_t):
    source_hot = jnp.concatenate([hot(source, 256 * k, 256) for k in range(4)], axis=0)
    gathered = nn(node_t[...], source_hot).astype(BF)
    kv = nn(wkv_t[...], gathered).astype(BF).astype(F32)
    pre = nn(wqe_t[...], jnp.concatenate([hot(target, 0, 256), edges_t], axis=0)) + kv[:256]
    gate = sigmoid(pre)
    new_edges = (edges_t.astype(F32) + pre * gate).astype(BF)
    return new_edges, gate * kv[256:]


def keep_weighted(weighted, target, position, count, at, hl, target_hot):
    top = weighted.astype(BF)
    hl[0:256, at] = top
    hl[256:512, at] = (weighted - top.astype(F32)).astype(BF)
    target_hot[:, at] = hot(jnp.where(position < count, target, -1), 0, 256)


def new_nodes(nodes_ref, acc, gain_ref):
    summed = (acc[0:256, :] + acc[256:512, :]).T
    centre = summed - jnp.mean(summed, axis=-1, keepdims=True)
    spread = jnp.mean(centre * centre, axis=-1, keepdims=True)
    normed = centre * lax.rsqrt(spread + 1e-05)
    return (nodes_ref[...].astype(F32) + gain_ref[...] * normed).astype(BF)


def first_kernel(
    count_ref, nodes_ref, before_ref, after_ref, low_ref, high_ref, wqkv_ref, wedge_ref, gain_ref, index_ref,
    src_ref, dst_ref, edge_ref,
    out_nodes_ref, c0_ref, c1_ref, out_edge_ref,
    node_t, wkv_t, wqe_t, acc, hl, target_hot,
):
    step = pl.program_id(0)
    count = count_ref[0]

    @pl.when(step == 0)
    def _():
        prepare(nodes_ref, before_ref, after_ref, low_ref, high_ref, wqkv_ref, wedge_ref, node_t, wkv_t, wqe_t)
        acc[...] = jnp.zeros_like(acc)

    @pl.when(step * BLOCK < count)
    def _():
        for j in range(BLOCK // SUB):
            at = slice(j * SUB, (j + 1) * SUB)
            target = dst_ref[0, :, at]
            position = step * BLOCK + j * SUB + lax.broadcasted_iota(jnp.int32, (1, SUB), 1)
            edges, weighted = edge_part(edge_ref[at, :].T, src_ref[0, :, at], target, node_t, wkv_t, wqe_t)
            out_edge_ref[0, :, at] = edges
            keep_weighted(weighted, target, position, count, at, hl, target_hot)
        acc[...] += nt(hl[...], target_hot[...])

    @pl.when(step == pl.num_programs(0) - 1)
    def _():
        nodes = new_nodes(nodes_ref, acc, gain_ref)
        out_nodes_ref[...] = nodes
        pick_corners(nodes, index_ref[...], c0_ref, c1_ref)


def second_kernel(
    count_ref, nodes_ref, before_ref, after_ref, low_ref, high_ref, wqkv_ref, wedge_ref, gain_ref,
    hin_ref, hout_ref, src_ref, dst_ref, edge_ref, goal_ref,
    out_nodes_ref, grad_ref,
    node_t, wkv_t, wqe_t, acc, hl, target_hot, hin_t, hout_t, edges_s, dact_s, hidden_s, dpred_s, grad_in, grad_out,
    *, scale,
):
    step = pl.program_id(0)
    count = count_ref[0]

    @pl.when(step == 0)
    def _():
        prepare(nodes_ref, before_ref, after_ref, low_ref, high_ref, wqkv_ref, wedge_ref, node_t, wkv_t, wqe_t)
        hin_t[...] = hin_ref[...].T
        hout_t[...] = hout_ref[...].T
        acc[...] = jnp.zeros_like(acc)
        grad_in[...] = jnp.zeros_like(grad_in)
        grad_out[...] = jnp.zeros_like(grad_out)

    @pl.when(step * BLOCK < count)
    def _():
        for j in range(BLOCK // SUB):
            at = slice(j * SUB, (j + 1) * SUB)
            target = dst_ref[0, :, at]
            position = step * BLOCK + j * SUB + lax.broadcasted_iota(jnp.int32, (1, SUB), 1)
            edges, weighted = edge_part(edge_ref[0, :, at], src_ref[0, :, at], target, node_t, wkv_t, wqe_t)
            edges_s[:, at] = edges
            keep_weighted(weighted, target, position, count, at, hl, target_hot)
            act = nn(hin_t[...], edges)
            gate = sigmoid(act)
            smooth = act * gate
            hidden = smooth.astype(BF)
            hidden_s[:, at] = hidden
            pred = nn(hout_t[...], hidden)
            weight = jnp.where(position < count, scale, 0.0)
            dpred = ((pred - goal_ref[:, at].astype(F32)) * weight).astype(BF)
            dpred_s[:, at] = dpred
            dhidden = nn(hout_ref[...], dpred)
            dact_s[:, at] = (dhidden * (gate + smooth * (1.0 - gate))).astype(BF)
        acc[...] += nt(hl[...], target_hot[...])
        grad_in[...] += nt(edges_s[...], dact_s[...])
        grad_out[...] += nt(hidden_s[...], dpred_s[...])

    @pl.when(step == pl.num_programs(0) - 1)
    def _():
        out_nodes_ref[...] = new_nodes(nodes_ref, acc, gain_ref)
        grad_ref[0] = grad_in[:, 0:128]
        grad_ref[1] = grad_in[:, 128:256]
        grad_ref[2] = grad_out[:, 0:128]
        grad_ref[3] = jnp.zeros((256, 128), F32)
        grad_ref[3, :, 0:41] = grad_out[:, 128:169]


def whole(*shape):
    return pl.BlockSpec(shape, lambda i: (0,) * len(shape))


COUNT = pl.BlockSpec(memory_space=pltpu.SMEM)
ROWS = pl.BlockSpec((1, 1, BLOCK), lambda i: (i, 0, 0))
EDGES_T = pl.BlockSpec((1, 256, BLOCK), lambda i: (i, 0, 0))
LAYER_SPECS = [
    COUNT, whole(256, 256), whole(2, 64, 256), whole(2, 64, 256), whole(4, 64, 256), whole(4, 64, 256),
    whole(256, 768), whole(256, 256), whole(1, 256),
]
LAYER_SCRATCH = [
    pltpu.VMEM((256, 1024), BF), pltpu.VMEM((512, 256), BF), pltpu.VMEM((256, 512), BF), pltpu.VMEM((512, 256), F32),
    pltpu.VMEM((512, BLOCK), BF), pltpu.VMEM((256, BLOCK), BF),
]
PARAMS = pltpu.CompilerParams(vmem_limit_bytes=48 * 2**20)
CORNER = jax.ShapeDtypeStruct((2, 64, 256), BF)


def halo(c0, c1):
    def both(low, high, axis):
        count = lax.axis_size(axis)
        up = [(i, (i + 1) % count) for i in range(count)]
        down = [(j, i) for i, j in up]
        return lax.ppermute(high, axis, up), lax.ppermute(low, axis, down)

    before, after = both(c0, c1, "gx")
    low, high = (jnp.stack([before[j], c0[j], c1[j], after[j]]) for j in range(2))
    return (before, after) + both(low, high, "gy")


def body(node_feat, edge_feat, edge_src, edge_dst, edge_count, send_idx, w_qkv, w_edge, gains, head_in, head_out, targets):
    slots = edge_feat.shape[0]
    blocks = slots // BLOCK
    scale = 0.125 / (slots * lax.axis_size(AXES)) ** 0.5
    index_row = send_idx.reshape(1, 256)
    source = edge_src.reshape(blocks, 1, BLOCK)
    target = edge_dst.reshape(blocks, 1, BLOCK)

    c0, c1 = pl.pallas_call(corner_kernel, out_shape=[CORNER, CORNER])(node_feat, index_row)
    nodes, c0, c1, edges = pl.pallas_call(
        first_kernel,
        grid=(blocks,),
        in_specs=LAYER_SPECS + [whole(1, 256), ROWS, ROWS, pl.BlockSpec((BLOCK, 256), lambda i: (i, 0))],
        out_specs=[whole(256, 256), whole(2, 64, 256), whole(2, 64, 256), EDGES_T],
        out_shape=[
            jax.ShapeDtypeStruct((256, 256), BF), CORNER, CORNER, jax.ShapeDtypeStruct((blocks, 256, BLOCK), BF),
        ],
        scratch_shapes=LAYER_SCRATCH,
        compiler_params=PARAMS,
    )(edge_count, node_feat, *halo(c0, c1), w_qkv[0], w_edge[0], gains[0:1], index_row, source, target, edge_feat)
    nodes, grads = pl.pallas_call(
        functools.partial(second_kernel, scale=scale),
        grid=(blocks,),
        in_specs=LAYER_SPECS + [
            whole(256, 256), whole(256, 169), ROWS, ROWS, EDGES_T, pl.BlockSpec((169, BLOCK), lambda i: (0, i)),
        ],
        out_specs=[whole(256, 256), whole(4, 256, 128)],
        out_shape=[jax.ShapeDtypeStruct((256, 256), BF), jax.ShapeDtypeStruct((4, 256, 128), F32)],
        scratch_shapes=LAYER_SCRATCH + [
            pltpu.VMEM((256, 256), BF), pltpu.VMEM((169, 256), BF), pltpu.VMEM((256, BLOCK), BF),
            pltpu.VMEM((256, BLOCK), BF), pltpu.VMEM((256, BLOCK), BF), pltpu.VMEM((169, BLOCK), BF),
            pltpu.VMEM((256, 256), F32), pltpu.VMEM((256, 169), F32),
        ],
        compiler_params=PARAMS,
    )(
        edge_count, nodes, *halo(c0, c1), w_qkv[1], w_edge[1], gains[1:2], head_in, head_out, source, target, edges, targets,
    )
    parts = lax.all_to_all(grads.reshape(128, 8, 128), AXES, 0, 0, tiled=True)
    share = jnp.sum(parts, axis=0)
    full = lax.all_to_all(jnp.broadcast_to(share[None], (128, 8, 128)), AXES, 0, 0, tiled=True).reshape(4, 256, 128)
    grad_in = jnp.concatenate([full[0], full[1]], axis=1)
    grad_out = jnp.concatenate([full[2], full[3, :, 0:41]], axis=1)
    return nodes, grad_in, grad_out


def solution(mesh):
    tile = P(AXES)
    return jax.shard_map(
        body,
        mesh=mesh,
        in_specs=(
            P(AXES, None), P(AXES, None), tile, tile, tile, P("rep", "gx", "gy", None, None, None),
            P(), P(), P(), P(), P(), P(None, AXES),
        ),
        out_specs=(P(AXES, None), P(), P()),
        check_vma=False,
    )
```

```python
import functools

import jax
import jax.numpy as jnp
from jax import lax
from jax.experimental import pallas as pl
from jax.experimental.pallas import tpu as pltpu
from jax.sharding import PartitionSpec as P

AXES = ("rep", "gx", "gy")
BF = jnp.bfloat16
F32 = jnp.float32
BLOCK = 2048
SUB = 256
LAGS = (1, 1, 1)
VMEM_MIB = 28


def nn(a, b):
    return jnp.dot(a, b, preferred_element_type=F32)


def nt(a, b):
    return lax.dot_general(a, b, (((1,), (1,)), ((), ())), preferred_element_type=F32)


def tn(a, b):
    return lax.dot_general(a, b, (((0,), (0,)), ((), ())), preferred_element_type=F32)


def hot(row, base, rows):
    index = lax.broadcasted_iota(jnp.int16, (rows, row.shape[1]), 0)
    same = index == (row - base).astype(jnp.int16)
    return jnp.where(same, jnp.ones((), BF), jnp.zeros((), BF))


def sigmoid(x):
    return 0.5 * jnp.tanh(0.5 * x) + 0.5


def pick_corners(nodes, index_ref, c0_ref, c1_ref):
    for i, out_ref in enumerate((c0_ref, c1_ref)):
        for j in range(2):
            out_ref[j] = tn(hot(index_ref[i, j : j + 1, :], 0, 256), nodes).astype(BF)


def corner_kernel(nodes_ref, index_ref, c0_ref, c1_ref):
    pick_corners(nodes_ref[...], index_ref, c0_ref, c1_ref)


def prepare(nodes_ref, before_ref, after_ref, low_ref, high_ref, wqkv_ref, wedge_ref, node_t, wkv_t, wqe_t):
    nodes = nodes_ref[...]
    cells = (
        low_ref[0], before_ref[0], before_ref[1], high_ref[0],
        low_ref[1], high_ref[1], low_ref[2], high_ref[2],
        low_ref[3], after_ref[0], after_ref[1], high_ref[3],
    )
    node_t[:, 0:256] = nodes.T
    for k in range(3):
        node_t[:, 256 * (k + 1) : 256 * (k + 2)] = jnp.concatenate(cells[4 * k : 4 * k + 4], axis=0).T
    wkv_t[...] = wqkv_ref[:, 256:].T
    wqe_t[:, 0:256] = nn(nodes, wqkv_ref[:, 0:256]).astype(BF).T
    wqe_t[:, 256:512] = wedge_ref[...].T


def new_nodes(nodes_ref, acc, gain):
    summed = (acc[0:256, :] + acc[256:512, :]).T
    centre = summed - jnp.mean(summed, axis=-1, keepdims=True)
    spread = jnp.mean(centre * centre, axis=-1, keepdims=True)
    normed = centre * lax.rsqrt(spread + 1e-05)
    return (nodes_ref[...].astype(F32) + gain * normed).astype(BF)


def staged(stages):
    parts = BLOCK // SUB
    held = [{} for _ in range(parts)]
    lag = 0
    lags = [lag := lag + step for _, step in stages]
    for tick in range(parts + lag):
        for (stage, _), late in zip(stages, lags):
            j = tick - late
            if 0 <= j < parts:
                stage(held[j], slice(j * SUB, (j + 1) * SUB), j * SUB)


def message_stages(first, count, src_ref, dst_ref, read_edges, node_t, wkv_t, wqe_t, hl, target_hot, keep_edges):
    def gather(held, at, start):
        source = src_ref[0, :, at]
        source_hot = jnp.concatenate([hot(source, 256 * k, 256) for k in range(4)], axis=0)
        held["rows"] = nn(node_t[...], source_hot).astype(BF)

    def message(held, at, start):
        target = dst_ref[0, :, at]
        edges = read_edges(at)
        kv = nn(wkv_t[...], held["rows"]).astype(BF).astype(F32)
        pre = nn(wqe_t[...], jnp.concatenate([hot(target, 0, 256), edges], axis=0)) + kv[:256]
        gate = sigmoid(pre)
        held["edges"] = (edges.astype(F32) + pre * gate).astype(BF)
        keep_edges(at, held["edges"])
        weighted = gate * kv[256:]
        top = weighted.astype(BF)
        hl[0:256, at] = top
        hl[256:512, at] = (weighted - top.astype(F32)).astype(BF)
        held["live"] = first + start + lax.broadcasted_iota(jnp.int32, (1, SUB), 1) < count
        target_hot[:, at] = hot(jnp.where(held["live"], target, -1), 0, 256)

    return [(gather, 0), (message, 1)]


def first_kernel(
    count_ref, nodes_ref, before_ref, after_ref, low_ref, high_ref, wqkv_ref, wedge_ref, gain_ref, index_ref,
    src_ref, dst_ref, edge_ref,
    out_nodes_ref, c0_ref, c1_ref, out_edge_ref,
    node_t, wkv_t, wqe_t, acc, hl, target_hot,
):
    step = pl.program_id(0)
    count = count_ref[0]

    @pl.when(step == 0)
    def _():
        prepare(nodes_ref, before_ref, after_ref, low_ref, high_ref, wqkv_ref, wedge_ref, node_t, wkv_t, wqe_t)
        acc[...] = jnp.zeros_like(acc)

    @pl.when(step * BLOCK < count)
    def _():
        def keep_edges(at, edges):
            out_edge_ref[0, :, at] = edges

        staged(
            message_stages(
                step * BLOCK, count, src_ref, dst_ref, lambda at: edge_ref[at, :].T, node_t, wkv_t, wqe_t, hl, target_hot,
                keep_edges,
            )
        )
        acc[...] += nt(hl[...], target_hot[...])

    @pl.when(step == pl.num_programs(0) - 1)
    def _():
        nodes = new_nodes(nodes_ref, acc, gain_ref[0:1, :])
        out_nodes_ref[...] = nodes
        pick_corners(nodes, index_ref, c0_ref, c1_ref)


def second_kernel(
    count_ref, nodes_ref, before_ref, after_ref, low_ref, high_ref, wqkv_ref, wedge_ref, gain_ref,
    hin_ref, hout_ref, src_ref, dst_ref, edge_ref, goal_ref,
    out_nodes_ref, grad_ref,
    node_t, wkv_t, wqe_t, acc, hl, target_hot, hin_t, hout, edges_s, dact_s, hidden_s, dpred_s, grad_in, grad_out,
    *, scale,
):
    step = pl.program_id(0)
    count = count_ref[0]

    @pl.when(step == 0)
    def _():
        prepare(nodes_ref, before_ref, after_ref, low_ref, high_ref, wqkv_ref, wedge_ref, node_t, wkv_t, wqe_t)
        hin_t[...] = hin_ref[...].T
        hout[...] = hout_ref[...].T
        acc[...] = jnp.zeros_like(acc)
        grad_in[...] = jnp.zeros_like(grad_in)
        grad_out[...] = jnp.zeros_like(grad_out)

    @pl.when(step * BLOCK < count)
    def _():
        def keep_edges(at, edges):
            edges_s[:, at] = edges

        def activate(held, at, start):
            act = nn(hin_t[...], held["edges"])
            gate = sigmoid(act)
            smooth = act * gate
            held["hidden"] = smooth.astype(BF)
            hidden_s[:, at] = held["hidden"]
            held["slope"] = gate + smooth * (1.0 - gate)

        def compare(held, at, start):
            pred = nn(hout_ref[...], held["hidden"])
            weight = jnp.where(held["live"], scale, 0.0)
            held["dpred"] = ((pred - goal_ref[:, at].astype(F32)) * weight).astype(BF)
            dpred_s[:, at] = held["dpred"]

        def back(held, at, start):
            dact_s[:, at] = (nn(hout[...], held["dpred"]) * held["slope"]).astype(BF)

        staged(
            message_stages(
                step * BLOCK, count, src_ref, dst_ref, lambda at: edge_ref[0, :, at], node_t, wkv_t, wqe_t, hl, target_hot,
                keep_edges,
            )
            + [(activate, LAGS[0]), (compare, LAGS[1]), (back, LAGS[2])]
        )
        acc[...] += nt(hl[...], target_hot[...])
        grad_in[...] += nt(edges_s[...], dact_s[...])
        grad_out[0:169, :] += nt(dpred_s[...], hidden_s[...])

    @pl.when(step == pl.num_programs(0) - 1)
    def _():
        out_nodes_ref[...] = new_nodes(nodes_ref, acc, gain_ref[1:2, :])
        tile = 0
        for total, rows in ((grad_in, 32), (grad_out, 22)):
            for i in range(rows):
                for j in range(2):
                    grad_ref[tile] = total[8 * i : 8 * i + 8, 128 * j : 128 * j + 128]
                    tile += 1
        grad_ref[tile:128] = jnp.zeros((128 - tile, 8, 128), F32)


def whole(*shape):
    return pl.BlockSpec(shape, lambda i: (0,) * len(shape))


def layer_specs(layer):
    return [
        pl.BlockSpec(memory_space=pltpu.SMEM),
        whole(256, 256), whole(2, 64, 256), whole(2, 64, 256), whole(4, 64, 256), whole(4, 64, 256),
        pl.BlockSpec((None, 256, 768), lambda i: (layer, 0, 0)), pl.BlockSpec((None, 256, 256), lambda i: (layer, 0, 0)),
        whole(2, 256),
    ]


ROWS = pl.BlockSpec((1, 1, BLOCK), lambda i: (i, 0, 0))
EDGES_T = pl.BlockSpec((1, 256, BLOCK), lambda i: (i, 0, 0))
LAYER_SCRATCH = [
    pltpu.VMEM((256, 1024), BF), pltpu.VMEM((512, 256), BF), pltpu.VMEM((256, 512), BF), pltpu.VMEM((512, 256), F32),
    pltpu.VMEM((512, BLOCK), BF), pltpu.VMEM((256, BLOCK), BF),
]
FIRST_PARAMS = pltpu.CompilerParams(vmem_limit_bytes=54 * 2**20)
PARAMS = pltpu.CompilerParams(vmem_limit_bytes=VMEM_MIB * 2**20)
CORNER = jax.ShapeDtypeStruct((2, 64, 256), BF)


def halo(c0, c1):
    def both(low, high, axis):
        count = lax.axis_size(axis)
        up = [(i, (i + 1) % count) for i in range(count)]
        down = [(j, i) for i, j in up]
        return lax.ppermute(high, axis, up), lax.ppermute(low, axis, down)

    before, after = both(c0, c1, "gx")
    low, high = (jnp.stack([before[j], c0[j], c1[j], after[j]]) for j in range(2))
    return (before, after) + both(low, high, "gy")


def body(node_feat, edge_feat, edge_src, edge_dst, edge_count, send_idx, w_qkv, w_edge, gains, head_in, head_out, targets):
    slots = edge_feat.shape[0]
    blocks = slots // BLOCK
    scale = 0.125 / (slots * lax.axis_size(AXES)) ** 0.5
    index = send_idx.reshape(2, 2, 64)
    source = edge_src.reshape(blocks, 1, BLOCK)
    target = edge_dst.reshape(blocks, 1, BLOCK)

    c0, c1 = pl.pallas_call(corner_kernel, out_shape=[CORNER, CORNER])(node_feat, index)
    nodes, c0, c1, edges = pl.pallas_call(
        first_kernel,
        grid=(blocks,),
        in_specs=layer_specs(0) + [whole(2, 2, 64), ROWS, ROWS, pl.BlockSpec((BLOCK, 256), lambda i: (i, 0))],
        out_specs=[whole(256, 256), whole(2, 64, 256), whole(2, 64, 256), EDGES_T],
        out_shape=[
            jax.ShapeDtypeStruct((256, 256), BF), CORNER, CORNER, jax.ShapeDtypeStruct((blocks, 256, BLOCK), BF),
        ],
        scratch_shapes=LAYER_SCRATCH,
        compiler_params=FIRST_PARAMS,
    )(edge_count, node_feat, *halo(c0, c1), w_qkv, w_edge, gains, index, source, target, edge_feat)
    nodes, grads = pl.pallas_call(
        functools.partial(second_kernel, scale=scale),
        grid=(blocks,),
        in_specs=layer_specs(1) + [
            whole(256, 256), whole(169, 256), ROWS, ROWS, EDGES_T, pl.BlockSpec((169, BLOCK), lambda i: (0, i)),
        ],
        out_specs=[whole(256, 256), whole(128, 8, 128)],
        out_shape=[jax.ShapeDtypeStruct((256, 256), BF), jax.ShapeDtypeStruct((128, 8, 128), F32)],
        scratch_shapes=LAYER_SCRATCH + [
            pltpu.VMEM((256, 256), BF), pltpu.VMEM((256, 169), BF), pltpu.VMEM((256, BLOCK), BF),
            pltpu.VMEM((256, BLOCK), BF), pltpu.VMEM((256, BLOCK), BF), pltpu.VMEM((169, BLOCK), BF),
            pltpu.VMEM((256, 256), F32), pltpu.VMEM((176, 256), F32),
        ],
        compiler_params=PARAMS,
    )(
        edge_count, nodes, *halo(c0, c1), w_qkv, w_edge, gains, head_in, head_out.T, source, target, edges, targets,
    )
    parts = lax.all_to_all(grads, AXES, 0, 0, tiled=True)
    share = jnp.sum(parts, axis=0)
    full = lax.all_to_all(jnp.broadcast_to(share[None], (128, 8, 128)), AXES, 0, 0, tiled=True)
    grad_in = full[0:64].reshape(32, 2, 8, 128).transpose(0, 2, 1, 3).reshape(256, 256)
    grad_out = full[64:108].reshape(22, 2, 8, 128).transpose(0, 2, 1, 3).reshape(176, 256)[0:169].T
    return nodes, grad_in, grad_out


def solution(mesh):
    tile = P(AXES)
    return jax.shard_map(
        body,
        mesh=mesh,
        in_specs=(
            P(AXES, None), P(AXES, None), tile, tile, tile, P("rep", "gx", "gy", None, None, None),
            P(), P(), P(), P(), P(), P(None, AXES),
        ),
        out_specs=(P(AXES, None), P(), P()),
        check_vma=False,
    )
```

```python
import functools

import jax
import jax.numpy as jnp
from jax import lax
from jax.experimental import pallas as pl
from jax.experimental.pallas import tpu as pltpu
from jax.sharding import PartitionSpec as P

AXES = ("rep", "gx", "gy")
BF = jnp.bfloat16
F32 = jnp.float32
BLOCK = 2048
SUB = 256
LAGS = (1, 1, 1)
VMEM_MIB = 28


def nn(a, b):
    return jnp.dot(a, b, preferred_element_type=F32)


def nt(a, b):
    return lax.dot_general(a, b, (((1,), (1,)), ((), ())), preferred_element_type=F32)


def tn(a, b):
    return lax.dot_general(a, b, (((0,), (0,)), ((), ())), preferred_element_type=F32)


def hot(row, base, rows):
    index = lax.broadcasted_iota(jnp.int16, (rows, row.shape[1]), 0)
    same = index == (row - base).astype(jnp.int16)
    return jnp.where(same, jnp.ones((), BF), jnp.zeros((), BF))


def sigmoid(x):
    return 0.5 * jnp.tanh(0.5 * x) + 0.5


def pick_corners(nodes, index_ref, c0_ref, c1_ref):
    for i, out_ref in enumerate((c0_ref, c1_ref)):
        for j in range(2):
            out_ref[j] = tn(hot(index_ref[i, j : j + 1, :], 0, 256), nodes).astype(BF)


def corner_kernel(nodes_ref, index_ref, c0_ref, c1_ref):
    pick_corners(nodes_ref[...], index_ref, c0_ref, c1_ref)


def stack_kernel(before_ref, after_ref, c0_ref, c1_ref, low_ref, high_ref):
    for j, out_ref in enumerate((low_ref, high_ref)):
        for i, cell_ref in enumerate((before_ref, c0_ref, c1_ref, after_ref)):
            out_ref[i] = cell_ref[j]


def prepare_own(nodes_ref, wqkv_ref, wedge_ref, node_t, wqe_t):
    nodes = nodes_ref[...]
    node_t[...] = nodes.T
    wqe_t[:, 0:256] = nn(nodes, wqkv_ref[:, 0:256]).astype(BF).T
    wqe_t[:, 256:512] = wedge_ref[...].T


def prepare_ghosts(before_ref, after_ref, low_ref, high_ref, wqkv_ref, ghost_t, wkv_t):
    cells = (
        low_ref[0], before_ref[0], before_ref[1], high_ref[0],
        low_ref[1], high_ref[1], low_ref[2], high_ref[2],
        low_ref[3], after_ref[0], after_ref[1], high_ref[3],
    )
    for k in range(3):
        ghost_t[:, 256 * k : 256 * (k + 1)] = jnp.concatenate(cells[4 * k : 4 * k + 4], axis=0).T
    wkv_t[...] = wqkv_ref[:, 256:].T


def new_nodes(nodes_ref, acc, gain):
    summed = (acc[0:256, :] + acc[256:512, :]).T
    centre = summed - jnp.mean(summed, axis=-1, keepdims=True)
    spread = jnp.mean(centre * centre, axis=-1, keepdims=True)
    normed = centre * lax.rsqrt(spread + 1e-05)
    return (nodes_ref[...].astype(F32) + gain * normed).astype(BF)


def staged(stages):
    parts = BLOCK // SUB
    held = [{} for _ in range(parts)]
    lag = 0
    lags = [lag := lag + step for _, step in stages]
    for tick in range(parts + lag):
        for (stage, _), late in zip(stages, lags):
            j = tick - late
            if 0 <= j < parts:
                stage(held[j], slice(j * SUB, (j + 1) * SUB), j * SUB)


def own_rows(at, source, target, edges, node_t, wqe_t, own_ref, part_ref):
    own_ref[0, :, at] = nn(node_t[...], hot(source, 0, 256)).astype(BF)
    part_ref[0, :, at] = nn(wqe_t[...], jnp.concatenate([hot(target, 0, 256), edges], axis=0))


def own_first_kernel(
    count_ref, nodes_hbm, wqkv_hbm, wedge_hbm, src_hbm, dst_hbm, edge_hbm, own_ref, part_ref, turned_ref,
    node_t, wqe_t, nodes, wqkv, wedge, src, dst, edge, sems,
):
    step = pl.program_id(0)
    steps = edge.shape[0]
    small = [
        pltpu.make_async_copy(nodes_hbm, nodes, sems.at[0]),
        pltpu.make_async_copy(wqkv_hbm.at[0, :, pl.ds(0, 256)], wqkv, sems.at[1]),
        pltpu.make_async_copy(wedge_hbm.at[0], wedge, sems.at[2]),
        pltpu.make_async_copy(src_hbm, src, sems.at[3]),
        pltpu.make_async_copy(dst_hbm, dst, sems.at[4]),
    ]

    def edge_copy(i):
        return pltpu.make_async_copy(edge_hbm.at[pl.ds(i * BLOCK, BLOCK), :], edge.at[i], sems.at[5 + i])

    @pl.when(step == 0)
    def _():
        for copy in small:
            copy.start()
        for i in range(steps):
            edge_copy(i).start()
        for copy in small:
            copy.wait()
        prepare_own(nodes, wqkv, wedge, node_t, wqe_t)

    edge_copy(step).wait()

    @pl.when(step * BLOCK < count_ref[0])
    def _():
        for j in range(BLOCK // SUB):
            at = slice(j * SUB, (j + 1) * SUB)
            edges = edge[step, at, :].T
            turned_ref[0, :, at] = edges
            own_rows(at, src[step, :, at], dst[step, :, at], edges, node_t, wqe_t, own_ref, part_ref)


def own_kernel(count_ref, nodes_ref, wqkv_ref, wedge_ref, src_ref, dst_ref, edge_ref, own_ref, part_ref, node_t, wqe_t):
    step = pl.program_id(0)

    @pl.when(step == 0)
    def _():
        prepare_own(nodes_ref, wqkv_ref, wedge_ref, node_t, wqe_t)

    @pl.when(step * BLOCK < count_ref[0])
    def _():
        for j in range(BLOCK // SUB):
            at = slice(j * SUB, (j + 1) * SUB)
            own_rows(at, src_ref[0, :, at], dst_ref[0, :, at], edge_ref[0, :, at], node_t, wqe_t, own_ref, part_ref)


def message_stages(first, count, src_ref, dst_ref, own_ref, part_ref, edge_ref, ghost_t, wkv_t, hl, target_hot, keep_edges):
    def gather(held, at, start):
        source = src_ref[0, :, at]
        source_hot = jnp.concatenate([hot(source, 256 * (k + 1), 256) for k in range(3)], axis=0)
        held["rows"] = nn(ghost_t[...], source_hot).astype(BF) + own_ref[0, :, at]

    def message(held, at, start):
        target = dst_ref[0, :, at]
        edges = edge_ref[0, :, at]
        kv = nn(wkv_t[...], held["rows"]).astype(BF).astype(F32)
        pre = part_ref[0, :, at] + kv[:256]
        gate = sigmoid(pre)
        held["edges"] = (edges.astype(F32) + pre * gate).astype(BF)
        keep_edges(at, held["edges"])
        weighted = gate * kv[256:]
        top = weighted.astype(BF)
        hl[0:256, at] = top
        hl[256:512, at] = (weighted - top.astype(F32)).astype(BF)
        held["live"] = first + start + lax.broadcasted_iota(jnp.int32, (1, SUB), 1) < count
        target_hot[:, at] = hot(jnp.where(held["live"], target, -1), 0, 256)

    return [(gather, 0), (message, 1)]


def first_kernel(
    count_ref, nodes_ref, before_ref, after_ref, low_ref, high_ref, wqkv_ref, gain_ref,
    src_ref, dst_ref, own_ref, part_ref, edge_ref, index_ref,
    out_nodes_ref, c0_ref, c1_ref, out_edge_ref,
    ghost_t, wkv_t, acc, hl, target_hot,
):
    step = pl.program_id(0)
    count = count_ref[0]

    @pl.when(step == 0)
    def _():
        prepare_ghosts(before_ref, after_ref, low_ref, high_ref, wqkv_ref, ghost_t, wkv_t)
        acc[...] = jnp.zeros_like(acc)

    @pl.when(step * BLOCK < count)
    def _():
        def keep_edges(at, edges):
            out_edge_ref[0, :, at] = edges

        staged(
            message_stages(
                step * BLOCK, count, src_ref, dst_ref, own_ref, part_ref, edge_ref, ghost_t, wkv_t, hl, target_hot, keep_edges
            )
        )
        acc[...] += nt(hl[...], target_hot[...])

    @pl.when(step == pl.num_programs(0) - 1)
    def _():
        nodes = new_nodes(nodes_ref, acc, gain_ref[0:1, :])
        out_nodes_ref[...] = nodes
        pick_corners(nodes, index_ref, c0_ref, c1_ref)


def second_kernel(
    count_ref, nodes_ref, before_ref, after_ref, low_ref, high_ref, wqkv_ref, gain_ref,
    src_ref, dst_ref, own_ref, part_ref, edge_ref, hin_ref, hout_ref, goal_ref,
    out_nodes_ref, grad_ref,
    ghost_t, wkv_t, acc, hl, target_hot, hin_t, hout, edges_s, dact_s, hidden_s, dpred_s, grad_in, grad_out,
    *, scale,
):
    step = pl.program_id(0)
    count = count_ref[0]

    @pl.when(step == 0)
    def _():
        prepare_ghosts(before_ref, after_ref, low_ref, high_ref, wqkv_ref, ghost_t, wkv_t)
        hin_t[...] = hin_ref[...].T
        hout[...] = hout_ref[...].T
        acc[...] = jnp.zeros_like(acc)
        grad_in[...] = jnp.zeros_like(grad_in)
        grad_out[...] = jnp.zeros_like(grad_out)

    @pl.when(step * BLOCK < count)
    def _():
        def keep_edges(at, edges):
            edges_s[:, at] = edges

        def activate(held, at, start):
            act = nn(hin_t[...], held["edges"])
            gate = sigmoid(act)
            smooth = act * gate
            held["hidden"] = smooth.astype(BF)
            hidden_s[:, at] = held["hidden"]
            held["slope"] = gate + smooth * (1.0 - gate)

        def compare(held, at, start):
            pred = nn(hout_ref[...], held["hidden"])
            weight = jnp.where(held["live"], scale, 0.0)
            held["dpred"] = ((pred - goal_ref[:, at].astype(F32)) * weight).astype(BF)
            dpred_s[:, at] = held["dpred"]

        def back(held, at, start):
            dact_s[:, at] = (nn(hout[...], held["dpred"]) * held["slope"]).astype(BF)

        staged(
            message_stages(
                step * BLOCK, count, src_ref, dst_ref, own_ref, part_ref, edge_ref, ghost_t, wkv_t, hl, target_hot, keep_edges
            )
            + [(activate, LAGS[0]), (compare, LAGS[1]), (back, LAGS[2])]
        )
        acc[...] += nt(hl[...], target_hot[...])
        grad_in[...] += nt(edges_s[...], dact_s[...])
        grad_out[0:169, :] += nt(dpred_s[...], hidden_s[...])

    @pl.when(step == pl.num_programs(0) - 1)
    def _():
        out_nodes_ref[...] = new_nodes(nodes_ref, acc, gain_ref[1:2, :])
        tile = 0
        for total, rows in ((grad_in, 32), (grad_out, 22)):
            for i in range(rows):
                for j in range(2):
                    grad_ref[tile] = total[8 * i : 8 * i + 8, 128 * j : 128 * j + 128]
                    tile += 1
        grad_ref[tile:128] = jnp.zeros((128 - tile, 8, 128), F32)


def whole(*shape):
    return pl.BlockSpec(shape, lambda i: (0,) * len(shape))


def layer_of(layer, *shape):
    return pl.BlockSpec((None,) + shape, lambda i: (layer, 0, 0))


SCALAR = pl.BlockSpec(memory_space=pltpu.SMEM)
ROWS = pl.BlockSpec((1, 1, BLOCK), lambda i: (i, 0, 0))
TURNED = pl.BlockSpec((1, 256, BLOCK), lambda i: (i, 0, 0))


def layer_specs(layer):
    return [
        SCALAR, whole(256, 256), whole(2, 64, 256), whole(2, 64, 256), whole(4, 64, 256), whole(4, 64, 256),
        layer_of(layer, 256, 768), whole(2, 256), ROWS, ROWS, TURNED, TURNED, TURNED,
    ]


LAYER_SCRATCH = [
    pltpu.VMEM((256, 768), BF), pltpu.VMEM((512, 256), BF), pltpu.VMEM((512, 256), F32),
    pltpu.VMEM((512, BLOCK), BF), pltpu.VMEM((256, BLOCK), BF),
]
SMALL = pltpu.CompilerParams(vmem_limit_bytes=4 * 2**20)
PARAMS = pltpu.CompilerParams(vmem_limit_bytes=VMEM_MIB * 2**20)
CORNER = jax.ShapeDtypeStruct((2, 64, 256), BF)


def stays(*arrays):
    return [pltpu.with_memory_space_constraint(x, pltpu.HBM) for x in arrays]


def halo(c0, c1):
    def both(low, high, axis):
        count = lax.axis_size(axis)
        up = [(i, (i + 1) % count) for i in range(count)]
        down = [(j, i) for i, j in up]
        return lax.ppermute(high, axis, up), lax.ppermute(low, axis, down)

    before, after = both(c0, c1, "gx")
    side = jax.ShapeDtypeStruct((4, 64, 256), BF)
    low, high = pl.pallas_call(stack_kernel, out_shape=[side, side], compiler_params=SMALL)(before, after, c0, c1)
    return (before, after) + both(low, high, "gy")


def body(node_feat, edge_feat, edge_src, edge_dst, edge_count, send_idx, w_qkv, w_edge, gains, head_in, head_out, targets):
    slots = edge_feat.shape[0]
    blocks = slots // BLOCK
    scale = 0.125 / (slots * lax.axis_size(AXES)) ** 0.5
    index = send_idx.reshape(2, 2, 64)
    source = edge_src.reshape(blocks, 1, BLOCK)
    target = edge_dst.reshape(blocks, 1, BLOCK)

    turned = jax.ShapeDtypeStruct((blocks, 256, BLOCK), BF)
    wide = jax.ShapeDtypeStruct((blocks, 256, BLOCK), F32)
    square = jax.ShapeDtypeStruct((256, 256), BF)

    weights = [pltpu.VMEM((256, 256), BF), pltpu.VMEM((256, 512), BF)]
    cost = pl.CostEstimate(flops=6 * slots * 65536, bytes_accessed=24 * 2**20, transcendentals=0)
    stay = pl.BlockSpec(memory_space=pltpu.HBM)

    def own_first(nodes):
        return pl.pallas_call(
            own_first_kernel,
            grid=(blocks,),
            in_specs=[SCALAR] + [stay] * 6,
            out_specs=[TURNED] * 3,
            out_shape=[turned, wide, turned],
            scratch_shapes=weights + [pltpu.VMEM((256, 256), BF)] * 3 + [pltpu.VMEM((blocks, 1, BLOCK), jnp.int32)] * 2
            + [pltpu.VMEM((blocks, BLOCK, 256), BF), pltpu.SemaphoreType.DMA((5 + blocks,))],
            compiler_params=PARAMS,
            cost_estimate=cost,
        )(edge_count, *stays(nodes, w_qkv, w_edge, source, target, edge_feat))

    def own_second(nodes, edges):
        return pl.pallas_call(
            own_kernel,
            grid=(blocks,),
            in_specs=[SCALAR, whole(256, 256), layer_of(1, 256, 256), layer_of(1, 256, 256), ROWS, ROWS, TURNED],
            out_specs=[TURNED] * 2,
            out_shape=[turned, wide],
            scratch_shapes=weights,
            compiler_params=PARAMS,
            cost_estimate=cost,
        )(edge_count, nodes, w_qkv, w_edge, source, target, edges)

    c0, c1 = pl.pallas_call(corner_kernel, out_shape=[CORNER, CORNER], compiler_params=SMALL)(*stays(node_feat, index))
    later_nodes, _ = lax.optimization_barrier((node_feat, c0))
    own, part, edges = own_first(later_nodes)
    nodes, c0, c1, edges = pl.pallas_call(
        first_kernel,
        grid=(blocks,),
        in_specs=layer_specs(0) + [whole(2, 2, 64)],
        out_specs=[whole(256, 256), whole(2, 64, 256), whole(2, 64, 256), TURNED],
        out_shape=[square, CORNER, CORNER, turned],
        scratch_shapes=LAYER_SCRATCH,
        compiler_params=PARAMS,
    )(edge_count, node_feat, *halo(c0, c1), w_qkv, gains, source, target, own, part, edges, index)
    own, part = own_second(nodes, edges)
    nodes, grads = pl.pallas_call(
        functools.partial(second_kernel, scale=scale),
        grid=(blocks,),
        in_specs=layer_specs(1) + [whole(256, 256), whole(169, 256), pl.BlockSpec((169, BLOCK), lambda i: (0, i))],
        out_specs=[whole(256, 256), whole(128, 8, 128)],
        out_shape=[square, jax.ShapeDtypeStruct((128, 8, 128), F32)],
        scratch_shapes=LAYER_SCRATCH + [
            pltpu.VMEM((256, 256), BF), pltpu.VMEM((256, 169), BF), pltpu.VMEM((256, BLOCK), BF),
            pltpu.VMEM((256, BLOCK), BF), pltpu.VMEM((256, BLOCK), BF), pltpu.VMEM((169, BLOCK), BF),
            pltpu.VMEM((256, 256), F32), pltpu.VMEM((176, 256), F32),
        ],
        compiler_params=PARAMS,
    )(
        edge_count, nodes, *halo(c0, c1), w_qkv, gains, source, target, own, part, edges, head_in, head_out.T, targets,
    )
    parts = lax.all_to_all(grads, AXES, 0, 0, tiled=True)
    share = jnp.sum(parts, axis=0)
    full = lax.all_to_all(jnp.broadcast_to(share[None], (128, 8, 128)), AXES, 0, 0, tiled=True)
    grad_in = full[0:64].reshape(32, 2, 8, 128).transpose(0, 2, 1, 3).reshape(256, 256)
    grad_out = full[64:108].reshape(22, 2, 8, 128).transpose(0, 2, 1, 3).reshape(176, 256)[0:169].T
    return nodes, grad_in, grad_out


def solution(mesh):
    tile = P(AXES)
    return jax.shard_map(
        body,
        mesh=mesh,
        in_specs=(
            P(AXES, None), P(AXES, None), tile, tile, tile, P("rep", "gx", "gy", None, None, None),
            P(), P(), P(), P(), P(), P(None, AXES),
        ),
        out_specs=(P(AXES, None), P(), P()),
        check_vma=False,
    )
```

```python
import functools

import jax
import jax.numpy as jnp
from jax import lax
from jax.experimental import pallas as pl
from jax.experimental.pallas import tpu as pltpu
from jax.sharding import Mesh
from jax.sharding import PartitionSpec as P

AXES = ("pair", "core", "gx", "gy")
BF = jnp.bfloat16
F32 = jnp.float32
BLOCK = 2048
SUB = 256
LAGS = (1, 1, 1)
VMEM_MIB = 28


def nn(a, b):
    return jnp.dot(a, b, preferred_element_type=F32)


def nt(a, b):
    return lax.dot_general(a, b, (((1,), (1,)), ((), ())), preferred_element_type=F32)


def tn(a, b):
    return lax.dot_general(a, b, (((0,), (0,)), ((), ())), preferred_element_type=F32)


def hot(row, base, rows):
    index = lax.broadcasted_iota(jnp.int16, (rows, row.shape[1]), 0)
    same = index == (row - base).astype(jnp.int16)
    return jnp.where(same, jnp.ones((), BF), jnp.zeros((), BF))


def sigmoid(x):
    return 0.5 * jnp.tanh(0.5 * x) + 0.5


def pick_corners(nodes, index_ref, c0_ref, c1_ref):
    for i, out_ref in enumerate((c0_ref, c1_ref)):
        for j in range(2):
            out_ref[j] = tn(hot(index_ref[i, j : j + 1, :], 0, 256), nodes).astype(BF)


def corner_kernel(nodes_ref, index_ref, c0_ref, c1_ref):
    pick_corners(nodes_ref[...], index_ref, c0_ref, c1_ref)


def stack_kernel(before_ref, after_ref, c0_ref, c1_ref, low_ref, high_ref):
    for j, out_ref in enumerate((low_ref, high_ref)):
        for i, cell_ref in enumerate((before_ref, c0_ref, c1_ref, after_ref)):
            out_ref[i] = cell_ref[j]


def prepare_own(nodes, wqkv, wedge, wqe_t):
    wqe_t[:, 0:256] = nn(nodes[...], wqkv[:, 0:256]).astype(BF).T
    wqe_t[:, 256:512] = wedge[...].T


def near_hot(source):
    return jnp.concatenate([hot(source, 0, 256), hot(source, 320, 128), hot(source, 832, 128)], axis=0)


def far_hot(source):
    return jnp.concatenate([hot(source, 256, 64), hot(source, 448, 384), hot(source, 960, 64)], axis=0)


def prepare_far(low_ref, high_ref, wqkv_ref, far_t, wkv_t):
    for k in range(2):
        cells = [low_ref[2 * k], high_ref[2 * k], low_ref[2 * k + 1], high_ref[2 * k + 1]]
        far_t[:, 256 * k : 256 * (k + 1)] = jnp.concatenate(cells, axis=0).T
    wkv_t[...] = wqkv_ref[:, 256:].T


def new_nodes(nodes_ref, acc, gain):
    summed = (acc[0:256, :] + acc[256:512, :]).T
    centre = summed - jnp.mean(summed, axis=-1, keepdims=True)
    spread = jnp.mean(centre * centre, axis=-1, keepdims=True)
    normed = centre * lax.rsqrt(spread + 1e-05)
    return (nodes_ref[...].astype(F32) + gain * normed).astype(BF)


def staged(stages):
    parts = BLOCK // SUB
    held = [{} for _ in range(parts)]
    lag = 0
    lags = [lag := lag + step for _, step in stages]
    for tick in range(parts + lag):
        for (stage, _), late in zip(stages, lags):
            j = tick - late
            if 0 <= j < parts:
                stage(held[j], slice(j * SUB, (j + 1) * SUB), j * SUB)


def part_of(target, edges, wqe_t):
    return nn(wqe_t[...], jnp.concatenate([hot(target, 0, 256), edges], axis=0))


def near_tables(nodes, before_ref, after_ref, near_t):
    near_t[:, 0:256] = nodes[...].T
    cells = [before_ref[0], before_ref[1], after_ref[0], after_ref[1]]
    near_t[:, 256:512] = jnp.concatenate(cells, axis=0).T


def first_part_kernel(
    count_ref, before_ref, after_ref, nodes_hbm, wqkv_hbm, wedge_hbm, src_hbm, dst_hbm, edge_hbm,
    near_ref, part_ref, turned_ref,
    near_t, wqe_t, nodes, wqkv, wedge, src, dst, edge, sems,
):
    step = pl.program_id(0)
    steps = edge.shape[0]
    small = [
        pltpu.make_async_copy(nodes_hbm, nodes, sems.at[0]),
        pltpu.make_async_copy(wqkv_hbm.at[0, :, pl.ds(0, 256)], wqkv, sems.at[1]),
        pltpu.make_async_copy(wedge_hbm.at[0], wedge, sems.at[2]),
        pltpu.make_async_copy(src_hbm, src, sems.at[3]),
        pltpu.make_async_copy(dst_hbm, dst, sems.at[4]),
    ]

    def edge_copy(i):
        return pltpu.make_async_copy(edge_hbm.at[pl.ds(i * BLOCK, BLOCK), :], edge.at[i], sems.at[5 + i])

    @pl.when(step == 0)
    def _():
        for copy in small:
            copy.start()
        for i in range(steps):
            edge_copy(i).start()
        for copy in small:
            copy.wait()
        prepare_own(nodes, wqkv, wedge, wqe_t)
        near_tables(nodes, before_ref, after_ref, near_t)

    edge_copy(step).wait()

    @pl.when(step * BLOCK < count_ref[0])
    def _():
        for j in range(BLOCK // SUB):
            at = slice(j * SUB, (j + 1) * SUB)
            near_ref[0, :, at] = nn(near_t[...], near_hot(src[step, :, at])).astype(BF)
            edges = edge[step, at, :].T
            turned_ref[0, :, at] = edges
            part_ref[0, :, at] = part_of(dst[step, :, at], edges, wqe_t)


def part_kernel(count_ref, nodes_ref, wqkv_ref, wedge_ref, dst_ref, edge_ref, part_ref, wqe_t):
    step = pl.program_id(0)

    @pl.when(step == 0)
    def _():
        prepare_own(nodes_ref, wqkv_ref, wedge_ref, wqe_t)

    @pl.when(step * BLOCK < count_ref[0])
    def _():
        for j in range(BLOCK // SUB):
            at = slice(j * SUB, (j + 1) * SUB)
            part_ref[0, :, at] = part_of(dst_ref[0, :, at], edge_ref[0, :, at], wqe_t)


def near_kernel(count_ref, nodes_ref, before_ref, after_ref, src_ref, near_ref, near_t):
    step = pl.program_id(0)

    @pl.when(step == 0)
    def _():
        near_tables(nodes_ref, before_ref, after_ref, near_t)

    @pl.when(step * BLOCK < count_ref[0])
    def _():
        for j in range(BLOCK // SUB):
            at = slice(j * SUB, (j + 1) * SUB)
            near_ref[0, :, at] = nn(near_t[...], near_hot(src_ref[0, :, at])).astype(BF)


def message_stages(first, count, src_ref, dst_ref, near_ref, part_ref, edge_ref, far_t, wkv_t, hl, target_hot, keep_edges):
    def gather(held, at, start):
        held["rows"] = nn(far_t[...], far_hot(src_ref[0, :, at])).astype(BF) + near_ref[0, :, at]

    def message(held, at, start):
        target = dst_ref[0, :, at]
        edges = edge_ref[0, :, at]
        kv = nn(wkv_t[...], held["rows"]).astype(BF).astype(F32)
        pre = part_ref[0, :, at] + kv[:256]
        gate = sigmoid(pre)
        held["edges"] = (edges.astype(F32) + pre * gate).astype(BF)
        keep_edges(at, held["edges"])
        weighted = gate * kv[256:]
        top = weighted.astype(BF)
        hl[0:256, at] = top
        hl[256:512, at] = (weighted - top.astype(F32)).astype(BF)
        held["live"] = first + start + lax.broadcasted_iota(jnp.int32, (1, SUB), 1) < count
        target_hot[:, at] = hot(jnp.where(held["live"], target, -1), 0, 256)

    return [(gather, 0), (message, 1)]


def first_kernel(
    count_ref, nodes_ref, low_ref, high_ref, wqkv_ref, gain_ref,
    src_ref, dst_ref, near_ref, part_ref, edge_ref, index_ref,
    out_nodes_ref, c0_ref, c1_ref, out_edge_ref,
    far_t, wkv_t, acc, hl, target_hot,
):
    step = pl.program_id(0)
    count = count_ref[0]

    @pl.when(step == 0)
    def _():
        prepare_far(low_ref, high_ref, wqkv_ref, far_t, wkv_t)
        acc[...] = jnp.zeros_like(acc)

    @pl.when(step * BLOCK < count)
    def _():
        def keep_edges(at, edges):
            out_edge_ref[0, :, at] = edges

        staged(
            message_stages(
                step * BLOCK, count, src_ref, dst_ref, near_ref, part_ref, edge_ref, far_t, wkv_t, hl, target_hot, keep_edges
            )
        )
        acc[...] += nt(hl[...], target_hot[...])

    @pl.when(step == pl.num_programs(0) - 1)
    def _():
        nodes = new_nodes(nodes_ref, acc, gain_ref[0:1, :])
        out_nodes_ref[...] = nodes
        pick_corners(nodes, index_ref, c0_ref, c1_ref)


def second_kernel(
    count_ref, nodes_ref, low_ref, high_ref, wqkv_ref, gain_ref,
    src_ref, dst_ref, near_ref, part_ref, edge_ref, core_ref, hin_ref, hout_ref, goal_ref,
    out_nodes_ref, keep_ref, send_ref,
    far_t, wkv_t, acc, hl, target_hot, hin_t, hout, edges_s, dact_s, hidden_s, dpred_s, grad_in, grad_out,
    *, scale,
):
    step = pl.program_id(0)
    count = count_ref[0]

    @pl.when(step == 0)
    def _():
        prepare_far(low_ref, high_ref, wqkv_ref, far_t, wkv_t)
        hin_t[...] = hin_ref[...].T
        hout[...] = hout_ref[...].T
        acc[...] = jnp.zeros_like(acc)
        grad_in[...] = jnp.zeros_like(grad_in)
        grad_out[...] = jnp.zeros_like(grad_out)

    @pl.when(step * BLOCK < count)
    def _():
        def keep_edges(at, edges):
            edges_s[:, at] = edges

        def activate(held, at, start):
            act = nn(hin_t[...], held["edges"])
            gate = sigmoid(act)
            smooth = act * gate
            held["hidden"] = smooth.astype(BF)
            hidden_s[:, at] = held["hidden"]
            held["slope"] = gate + smooth * (1.0 - gate)

        def compare(held, at, start):
            pred = nn(hout_ref[...], held["hidden"])
            weight = jnp.where(held["live"], scale, 0.0)
            held["dpred"] = ((pred - goal_ref[:, at].astype(F32)) * weight).astype(BF)
            dpred_s[:, at] = held["dpred"]

        def back(held, at, start):
            dact_s[:, at] = (nn(hout[...], held["dpred"]) * held["slope"]).astype(BF)

        staged(
            message_stages(
                step * BLOCK, count, src_ref, dst_ref, near_ref, part_ref, edge_ref, far_t, wkv_t, hl, target_hot, keep_edges
            )
            + [(activate, LAGS[0]), (compare, LAGS[1]), (back, LAGS[2])]
        )
        acc[...] += nt(hl[...], target_hot[...])
        grad_in[...] += nt(edges_s[...], dact_s[...])
        grad_out[0:169, :] += nt(dpred_s[...], hidden_s[...])

    @pl.when(step == pl.num_programs(0) - 1)
    def _():
        out_nodes_ref[...] = new_nodes(nodes_ref, acc, gain_ref[1:2, :])

        def tiles_to(total, rows, to_ref):
            for i in range(rows):
                for j in range(2):
                    to_ref[2 * i + j] = total[8 * i : 8 * i + 8, 128 * j : 128 * j + 128]
            if rows < 32:
                to_ref[2 * rows : 64] = jnp.zeros((64 - 2 * rows, 8, 128), F32)

        @pl.when(core_ref[0] == 0)
        def _():
            tiles_to(grad_in, 32, keep_ref)
            tiles_to(grad_out, 22, send_ref)

        @pl.when(core_ref[0] == 1)
        def _():
            tiles_to(grad_out, 22, keep_ref)
            tiles_to(grad_in, 32, send_ref)


def whole(*shape):
    return pl.BlockSpec(shape, lambda i: (0,) * len(shape))


def layer_of(layer, *shape):
    return pl.BlockSpec((None,) + shape, lambda i: (layer, 0, 0))


SCALAR = pl.BlockSpec(memory_space=pltpu.SMEM)
ROWS = pl.BlockSpec((1, 1, BLOCK), lambda i: (i, 0, 0))
TURNED = pl.BlockSpec((1, 256, BLOCK), lambda i: (i, 0, 0))


def layer_specs(layer):
    return [
        SCALAR, whole(256, 256), whole(4, 64, 256), whole(4, 64, 256),
        layer_of(layer, 256, 768), whole(2, 256), ROWS, ROWS, TURNED, TURNED, TURNED,
    ]


LAYER_SCRATCH = [
    pltpu.VMEM((256, 512), BF), pltpu.VMEM((512, 256), BF), pltpu.VMEM((512, 256), F32),
    pltpu.VMEM((512, BLOCK), BF), pltpu.VMEM((256, BLOCK), BF),
]
LIGHT = pltpu.CompilerParams(vmem_limit_bytes=16 * 2**20)
SMALL = pltpu.CompilerParams(vmem_limit_bytes=4 * 2**20)
PARAMS = pltpu.CompilerParams(vmem_limit_bytes=VMEM_MIB * 2**20)
CORNER = jax.ShapeDtypeStruct((2, 64, 256), BF)


def stays(*arrays):
    return [pltpu.with_memory_space_constraint(x, pltpu.HBM) for x in arrays]


def shift(low, high, axis):
    count = lax.axis_size(axis)
    up = [(i, (i + 1) % count) for i in range(count)]
    down = [(j, i) for i, j in up]
    return lax.ppermute(high, axis, up), lax.ppermute(low, axis, down)


def turn_sides(before, after, c0, c1):
    side = jax.ShapeDtypeStruct((4, 64, 256), BF)
    low, high = pl.pallas_call(stack_kernel, out_shape=[side, side], compiler_params=SMALL)(before, after, c0, c1)
    return shift(low, high, "gy")


def swap_cores(x):
    return lax.ppermute(x, "core", [(0, 1), (1, 0)])


def body(node_feat, edge_feat, edge_src, edge_dst, edge_count, send_idx, w_qkv, w_edge, gains, head_in, head_out, targets):
    slots = edge_feat.shape[0]
    blocks = slots // BLOCK
    scale = 0.125 / (slots * lax.axis_size(AXES)) ** 0.5
    index = send_idx.reshape(2, 2, 64)
    source = edge_src.reshape(blocks, 1, BLOCK)
    target = edge_dst.reshape(blocks, 1, BLOCK)

    turned = jax.ShapeDtypeStruct((blocks, 256, BLOCK), BF)
    wide = jax.ShapeDtypeStruct((blocks, 256, BLOCK), F32)
    square = jax.ShapeDtypeStruct((256, 256), BF)

    def cost(units):
        return pl.CostEstimate(flops=2 * units * slots * 65536, bytes_accessed=units * 6 * 2**20, transcendentals=0)

    def first_part(before, after):
        stay = pl.BlockSpec(memory_space=pltpu.HBM)
        index_rows = pltpu.VMEM((blocks, 1, BLOCK), jnp.int32)
        return pl.pallas_call(
            first_part_kernel,
            grid=(blocks,),
            in_specs=[SCALAR, whole(2, 64, 256), whole(2, 64, 256)] + [stay] * 6,
            out_specs=[TURNED] * 3,
            out_shape=[turned, wide, turned],
            scratch_shapes=[pltpu.VMEM((256, 512), BF)] * 2 + [pltpu.VMEM((256, 256), BF)] * 3
            + [index_rows, index_rows, pltpu.VMEM((blocks, BLOCK, 256), BF), pltpu.SemaphoreType.DMA((5 + blocks,))],
            compiler_params=PARAMS,
            cost_estimate=cost(4),
        )(edge_count, before, after, *stays(node_feat, w_qkv, w_edge, source, target, edge_feat))

    def second_part(nodes, edges):
        return pl.pallas_call(
            part_kernel,
            grid=(blocks,),
            in_specs=[SCALAR, whole(256, 256), layer_of(1, 256, 256), layer_of(1, 256, 256), ROWS, TURNED],
            out_specs=TURNED,
            out_shape=wide,
            scratch_shapes=[pltpu.VMEM((256, 512), BF)],
            compiler_params=LIGHT,
            cost_estimate=cost(2),
        )(edge_count, nodes, w_qkv, w_edge, target, edges)

    def near(nodes, before, after):
        return pl.pallas_call(
            near_kernel,
            grid=(blocks,),
            in_specs=[SCALAR, whole(256, 256), whole(2, 64, 256), whole(2, 64, 256), ROWS],
            out_specs=TURNED,
            out_shape=turned,
            scratch_shapes=[pltpu.VMEM((256, 512), BF)],
            compiler_params=LIGHT,
            cost_estimate=cost(2),
        )(edge_count, nodes, before, after, source)

    c0, c1 = pl.pallas_call(corner_kernel, out_shape=[CORNER, CORNER], compiler_params=SMALL)(*stays(node_feat, index))
    before, after = shift(c0, c1, "gx")
    low, high = turn_sides(before, after, c0, c1)
    rows, part, edges = first_part(before, after)
    nodes, c0, c1, edges = pl.pallas_call(
        first_kernel,
        grid=(blocks,),
        in_specs=layer_specs(0) + [whole(2, 2, 64)],
        out_specs=[whole(256, 256), whole(2, 64, 256), whole(2, 64, 256), TURNED],
        out_shape=[square, CORNER, CORNER, turned],
        scratch_shapes=LAYER_SCRATCH,
        compiler_params=PARAMS,
    )(edge_count, node_feat, low, high, w_qkv, gains, source, target, rows, part, edges, index)

    before, after = shift(c0, c1, "gx")
    part = second_part(nodes, edges)
    before, after, part = lax.optimization_barrier((before, after, part))
    low, high = turn_sides(before, after, c0, c1)
    rows = near(nodes, before, after)
    half = jax.ShapeDtypeStruct((64, 8, 128), F32)
    core = lax.axis_index("core")
    nodes, keep, send = pl.pallas_call(
        functools.partial(second_kernel, scale=scale),
        grid=(blocks,),
        in_specs=layer_specs(1) + [SCALAR, whole(256, 256), whole(169, 256), pl.BlockSpec((169, BLOCK), lambda i: (0, i))],
        out_specs=[whole(256, 256), whole(64, 8, 128), whole(64, 8, 128)],
        out_shape=[square, half, half],
        scratch_shapes=LAYER_SCRATCH + [
            pltpu.VMEM((256, 256), BF), pltpu.VMEM((256, 169), BF), pltpu.VMEM((256, BLOCK), BF),
            pltpu.VMEM((256, BLOCK), BF), pltpu.VMEM((256, BLOCK), BF), pltpu.VMEM((169, BLOCK), BF),
            pltpu.VMEM((256, 256), F32), pltpu.VMEM((176, 256), F32),
        ],
        compiler_params=PARAMS,
    )(
        edge_count, nodes, low, high, w_qkv, gains, source, target, rows, part, edges,
        core.astype(jnp.int32).reshape(1), head_in, head_out.T, targets,
    )
    chips = ("pair", "gx", "gy")
    parts = lax.all_to_all(keep + swap_cores(send), chips, 0, 0, tiled=True)
    share = jnp.sum(parts, axis=0)
    mine = lax.all_to_all(jnp.broadcast_to(share[None], (64, 8, 128)), chips, 0, 0, tiled=True)
    other = swap_cores(mine)
    grad_in = jnp.where(core == 0, mine, other)
    grad_out = jnp.where(core == 0, other, mine)[0:44]
    grad_in = grad_in.reshape(32, 2, 8, 128).transpose(0, 2, 1, 3).reshape(256, 256)
    grad_out = grad_out.reshape(22, 2, 8, 128).transpose(0, 2, 1, 3).reshape(176, 256)[0:169].T
    return nodes, grad_in, grad_out


def solution(mesh):
    shape = dict(mesh.shape)
    cut = Mesh(mesh.devices.reshape(shape["rep"] // 2, 2, shape["gx"], shape["gy"]), AXES)
    tile = P(AXES)
    return jax.shard_map(
        body,
        mesh=cut,
        in_specs=(
            P(AXES, None), P(AXES, None), tile, tile, tile, P(("pair", "core"), "gx", "gy", None, None, None),
            P(), P(), P(), P(), P(), P(None, AXES),
        ),
        out_specs=(P(AXES, None), P(), P()),
        check_vma=False,
    )
```

```python
import functools

import jax
import jax.numpy as jnp
from jax import lax
from jax.experimental import pallas as pl
from jax.experimental.pallas import tpu as pltpu
from jax.sharding import Mesh
from jax.sharding import PartitionSpec as P

AXES = ("pair", "core", "gx", "gy")
BF = jnp.bfloat16
F32 = jnp.float32
BLOCK = 2048
SUB = 256
LAGS = (1, 1, 1)
VMEM_MIB = 28


def nn(a, b):
    return jnp.dot(a, b, preferred_element_type=F32)


def nt(a, b):
    return lax.dot_general(a, b, (((1,), (1,)), ((), ())), preferred_element_type=F32)


def tn(a, b):
    return lax.dot_general(a, b, (((0,), (0,)), ((), ())), preferred_element_type=F32)


def hot(row, base, rows):
    index = lax.broadcasted_iota(jnp.int16, (rows, row.shape[1]), 0)
    same = index == (row - base).astype(jnp.int16)
    return jnp.where(same, jnp.ones((), BF), jnp.zeros((), BF))


def sigmoid(x):
    return 0.5 * jnp.tanh(0.5 * x) + 0.5


def pick_corners(nodes, index_ref, c0_ref, c1_ref):
    for i, out_ref in enumerate((c0_ref, c1_ref)):
        for j in range(2):
            out_ref[j] = tn(hot(index_ref[i, j : j + 1, :], 0, 256), nodes).astype(BF)


def corner_kernel(nodes_ref, index_ref, c0_ref, c1_ref):
    pick_corners(nodes_ref[...], index_ref, c0_ref, c1_ref)


def stack_kernel(before_ref, after_ref, c0_ref, c1_ref, low_ref, high_ref):
    for j, out_ref in enumerate((low_ref, high_ref)):
        for i, cell_ref in enumerate((before_ref, c0_ref, c1_ref, after_ref)):
            out_ref[i] = cell_ref[j]


def prepare_own(nodes, wqkv, wedge, wqe_t):
    wqe_t[:, 0:256] = nn(nodes[...], wqkv[:, 0:256]).astype(BF).T
    wqe_t[:, 256:512] = wedge[...].T


def near_hot(source):
    return jnp.concatenate([hot(source, 0, 256), hot(source, 320, 128), hot(source, 832, 128)], axis=0)


def far_hot(source):
    return jnp.concatenate([hot(source, 256, 64), hot(source, 448, 384), hot(source, 960, 64)], axis=0)


def prepare_far(low_ref, high_ref, wqkv_ref, far_t, wkv_t):
    for k in range(2):
        cells = [low_ref[2 * k], high_ref[2 * k], low_ref[2 * k + 1], high_ref[2 * k + 1]]
        far_t[:, 256 * k : 256 * (k + 1)] = jnp.concatenate(cells, axis=0).T
    wkv_t[...] = wqkv_ref[:, 256:].T


def new_nodes(nodes_ref, acc, gain):
    summed = (acc[0:256, :] + acc[256:512, :]).T
    centre = summed - jnp.mean(summed, axis=-1, keepdims=True)
    spread = jnp.mean(centre * centre, axis=-1, keepdims=True)
    normed = centre * lax.rsqrt(spread + 1e-05)
    return (nodes_ref[...].astype(F32) + gain * normed).astype(BF)


def staged(stages):
    parts = BLOCK // SUB
    held = [{} for _ in range(parts)]
    lag = 0
    lags = [lag := lag + step for _, step in stages]
    for tick in range(parts + lag):
        for (stage, _), late in zip(stages, lags):
            j = tick - late
            if 0 <= j < parts:
                stage(held[j], slice(j * SUB, (j + 1) * SUB), j * SUB)


def part_of(target, edges, wqe_t):
    return nn(wqe_t[...], jnp.concatenate([hot(target, 0, 256), edges], axis=0))


def near_tables(nodes, before_ref, after_ref, near_t):
    near_t[:, 0:256] = nodes[...].T
    cells = [before_ref[0], before_ref[1], after_ref[0], after_ref[1]]
    near_t[:, 256:512] = jnp.concatenate(cells, axis=0).T


def first_part_kernel(
    count_ref, before_ref, after_ref, nodes_hbm, wqkv_hbm, wedge_hbm, src_hbm, dst_hbm, edge_hbm,
    near_ref, part_ref, turned_ref,
    near_t, wqe_t, nodes, wqkv, wedge, src, dst, edge, sems,
):
    step = pl.program_id(0)
    steps = edge.shape[0]
    small = [
        pltpu.make_async_copy(nodes_hbm, nodes, sems.at[0]),
        pltpu.make_async_copy(wqkv_hbm.at[0, :, pl.ds(0, 256)], wqkv, sems.at[1]),
        pltpu.make_async_copy(wedge_hbm.at[0], wedge, sems.at[2]),
        pltpu.make_async_copy(src_hbm, src, sems.at[3]),
        pltpu.make_async_copy(dst_hbm, dst, sems.at[4]),
    ]

    def edge_copy(i):
        return pltpu.make_async_copy(edge_hbm.at[pl.ds(i * BLOCK, BLOCK), :], edge.at[i], sems.at[5 + i])

    @pl.when(step == 0)
    def _():
        for copy in small:
            copy.start()
        for i in range(steps):
            edge_copy(i).start()
        for copy in small:
            copy.wait()
        prepare_own(nodes, wqkv, wedge, wqe_t)
        near_tables(nodes, before_ref, after_ref, near_t)

    edge_copy(step).wait()

    @pl.when(step * BLOCK < count_ref[0])
    def _():
        for j in range(BLOCK // SUB):
            at = slice(j * SUB, (j + 1) * SUB)
            near_ref[0, :, at] = nn(near_t[...], near_hot(src[step, :, at])).astype(BF)
            edges = edge[step, at, :].T
            turned_ref[0, :, at] = edges
            part_ref[0, :, at] = part_of(dst[step, :, at], edges, wqe_t)


def part_kernel(count_ref, nodes_ref, wqkv_ref, wedge_ref, dst_ref, edge_ref, part_ref, wqe_t):
    step = pl.program_id(0)

    @pl.when(step == 0)
    def _():
        prepare_own(nodes_ref, wqkv_ref, wedge_ref, wqe_t)

    @pl.when(step * BLOCK < count_ref[0])
    def _():
        for j in range(BLOCK // SUB):
            at = slice(j * SUB, (j + 1) * SUB)
            part_ref[0, :, at] = part_of(dst_ref[0, :, at], edge_ref[0, :, at], wqe_t)


def near_kernel(count_ref, nodes_ref, before_ref, after_ref, src_ref, near_ref, near_t):
    step = pl.program_id(0)

    @pl.when(step == 0)
    def _():
        near_tables(nodes_ref, before_ref, after_ref, near_t)

    @pl.when(step * BLOCK < count_ref[0])
    def _():
        for j in range(BLOCK // SUB):
            at = slice(j * SUB, (j + 1) * SUB)
            near_ref[0, :, at] = nn(near_t[...], near_hot(src_ref[0, :, at])).astype(BF)


def message_stages(first, count, src_ref, dst_ref, near_ref, part_ref, edge_ref, far_t, wkv_t, hl, target_hot, keep_edges, lag):
    def gather(held, at, start):
        held["rows"] = nn(far_t[...], far_hot(src_ref[0, :, at])).astype(BF) + near_ref[0, :, at]

    def message(held, at, start):
        target = dst_ref[0, :, at]
        edges = edge_ref[0, :, at]
        kv = nn(wkv_t[...], held["rows"]).astype(BF).astype(F32)
        pre = part_ref[0, :, at] + kv[:256]
        gate = sigmoid(pre)
        held["edges"] = (edges.astype(F32) + pre * gate).astype(BF)
        keep_edges(at, held["edges"])
        weighted = gate * kv[256:]
        top = weighted.astype(BF)
        hl[0:256, at] = top
        hl[256:512, at] = (weighted - top.astype(F32)).astype(BF)
        held["live"] = first + start + lax.broadcasted_iota(jnp.int32, (1, SUB), 1) < count
        target_hot[:, at] = hot(jnp.where(held["live"], target, -1), 0, 256)

    return [(gather, 0), (message, lag)]


def first_kernel(
    count_ref, nodes_ref, low_ref, high_ref, wqkv_ref, gain_ref,
    src_ref, dst_ref, near_ref, part_ref, edge_ref, index_ref,
    out_nodes_ref, c0_ref, c1_ref, out_edge_ref,
    far_t, wkv_t, acc, hl, target_hot,
):
    step = pl.program_id(0)
    count = count_ref[0]

    @pl.when(step == 0)
    def _():
        prepare_far(low_ref, high_ref, wqkv_ref, far_t, wkv_t)
        acc[...] = jnp.zeros_like(acc)

    @pl.when(step * BLOCK < count)
    def _():
        def keep_edges(at, edges):
            out_edge_ref[0, :, at] = edges

        staged(
            message_stages(
                step * BLOCK, count, src_ref, dst_ref, near_ref, part_ref, edge_ref, far_t, wkv_t, hl, target_hot, keep_edges, 0
            )
        )
        acc[...] += nt(hl[...], target_hot[...])

    @pl.when(step == pl.num_programs(0) - 1)
    def _():
        nodes = new_nodes(nodes_ref, acc, gain_ref[0:1, :])
        out_nodes_ref[...] = nodes
        pick_corners(nodes, index_ref, c0_ref, c1_ref)


def second_kernel(
    count_ref, nodes_ref, low_ref, high_ref, wqkv_ref, gain_ref,
    src_ref, dst_ref, near_ref, part_ref, edge_ref, core_ref, hin_ref, hout_ref, goal_ref,
    out_nodes_ref, keep_ref, send_ref,
    far_t, wkv_t, acc, hl, target_hot, hin_t, hout, edges_s, dact_s, hidden_s, dpred_s, grad_in, grad_out,
    *, scale,
):
    step = pl.program_id(0)
    count = count_ref[0]

    @pl.when(step == 0)
    def _():
        prepare_far(low_ref, high_ref, wqkv_ref, far_t, wkv_t)
        hin_t[...] = hin_ref[...].T
        hout[...] = hout_ref[...].T
        acc[...] = jnp.zeros_like(acc)
        grad_in[...] = jnp.zeros_like(grad_in)
        grad_out[...] = jnp.zeros_like(grad_out)

    @pl.when(step * BLOCK < count)
    def _():
        def keep_edges(at, edges):
            edges_s[:, at] = edges

        def activate(held, at, start):
            act = nn(hin_t[...], held["edges"])
            gate = sigmoid(act)
            smooth = act * gate
            held["hidden"] = smooth.astype(BF)
            hidden_s[:, at] = held["hidden"]
            held["slope"] = gate + smooth * (1.0 - gate)

        def compare(held, at, start):
            pred = nn(hout_ref[...], held["hidden"])
            weight = jnp.where(held["live"], scale, 0.0)
            held["dpred"] = ((pred - goal_ref[:, at].astype(F32)) * weight).astype(BF)
            dpred_s[:, at] = held["dpred"]

        def back(held, at, start):
            dact_s[:, at] = (nn(hout[...], held["dpred"]) * held["slope"]).astype(BF)

        staged(
            message_stages(
                step * BLOCK, count, src_ref, dst_ref, near_ref, part_ref, edge_ref, far_t, wkv_t, hl, target_hot, keep_edges, 1
            )
            + [(activate, LAGS[0]), (compare, LAGS[1]), (back, LAGS[2])]
        )
        acc[...] += nt(hl[...], target_hot[...])
        grad_in[...] += nt(edges_s[...], dact_s[...])
        grad_out[0:169, :] += nt(dpred_s[...], hidden_s[...])

    @pl.when(step == pl.num_programs(0) - 1)
    def _():
        out_nodes_ref[...] = new_nodes(nodes_ref, acc, gain_ref[1:2, :])

        def tiles_to(total, rows, to_ref):
            for i in range(rows):
                for j in range(2):
                    to_ref[2 * i + j] = total[8 * i : 8 * i + 8, 128 * j : 128 * j + 128]
            if rows < 32:
                to_ref[2 * rows : 64] = jnp.zeros((64 - 2 * rows, 8, 128), F32)

        @pl.when(core_ref[0] == 0)
        def _():
            tiles_to(grad_in, 32, keep_ref)
            tiles_to(grad_out, 22, send_ref)

        @pl.when(core_ref[0] == 1)
        def _():
            tiles_to(grad_out, 22, keep_ref)
            tiles_to(grad_in, 32, send_ref)


def whole(*shape):
    return pl.BlockSpec(shape, lambda i: (0,) * len(shape))


def layer_of(layer, *shape):
    return pl.BlockSpec((None,) + shape, lambda i: (layer, 0, 0))


SCALAR = pl.BlockSpec(memory_space=pltpu.SMEM)
ROWS = pl.BlockSpec((1, 1, BLOCK), lambda i: (i, 0, 0))
TURNED = pl.BlockSpec((1, 256, BLOCK), lambda i: (i, 0, 0))


def layer_specs(layer):
    return [
        SCALAR, whole(256, 256), whole(4, 64, 256), whole(4, 64, 256),
        layer_of(layer, 256, 768), whole(2, 256), ROWS, ROWS, TURNED, TURNED, TURNED,
    ]


LAYER_SCRATCH = [
    pltpu.VMEM((256, 512), BF), pltpu.VMEM((512, 256), BF), pltpu.VMEM((512, 256), F32),
    pltpu.VMEM((512, BLOCK), BF), pltpu.VMEM((256, BLOCK), BF),
]
LIGHT = pltpu.CompilerParams(vmem_limit_bytes=16 * 2**20)
SMALL = pltpu.CompilerParams(vmem_limit_bytes=4 * 2**20)
PARAMS = pltpu.CompilerParams(vmem_limit_bytes=VMEM_MIB * 2**20)
CORNER = jax.ShapeDtypeStruct((2, 64, 256), BF)


def stays(*arrays):
    return [pltpu.with_memory_space_constraint(x, pltpu.HBM) for x in arrays]


def shift(low, high, axis):
    count = lax.axis_size(axis)
    up = [(i, (i + 1) % count) for i in range(count)]
    down = [(j, i) for i, j in up]
    return lax.ppermute(high, axis, up), lax.ppermute(low, axis, down)


def turn_sides(before, after, c0, c1):
    side = jax.ShapeDtypeStruct((4, 64, 256), BF)
    low, high = pl.pallas_call(stack_kernel, out_shape=[side, side], compiler_params=SMALL)(before, after, c0, c1)
    return shift(low, high, "gy")


def swap_cores(x):
    return lax.ppermute(x, "core", [(0, 1), (1, 0)])


def body(node_feat, edge_feat, edge_src, edge_dst, edge_count, send_idx, w_qkv, w_edge, gains, head_in, head_out, targets):
    slots = edge_feat.shape[0]
    blocks = slots // BLOCK
    scale = 0.125 / (slots * lax.axis_size(AXES)) ** 0.5
    index = send_idx.reshape(2, 2, 64)
    source = edge_src.reshape(blocks, 1, BLOCK)
    target = edge_dst.reshape(blocks, 1, BLOCK)

    turned = jax.ShapeDtypeStruct((blocks, 256, BLOCK), BF)
    wide = jax.ShapeDtypeStruct((blocks, 256, BLOCK), F32)
    square = jax.ShapeDtypeStruct((256, 256), BF)

    def cost(units):
        return pl.CostEstimate(flops=2 * units * slots * 65536, bytes_accessed=units * 6 * 2**20, transcendentals=0)

    def first_part(before, after):
        stay = pl.BlockSpec(memory_space=pltpu.HBM)
        index_rows = pltpu.VMEM((blocks, 1, BLOCK), jnp.int32)
        return pl.pallas_call(
            first_part_kernel,
            grid=(blocks,),
            in_specs=[SCALAR, whole(2, 64, 256), whole(2, 64, 256)] + [stay] * 6,
            out_specs=[TURNED] * 3,
            out_shape=[turned, wide, turned],
            scratch_shapes=[pltpu.VMEM((256, 512), BF)] * 2 + [pltpu.VMEM((256, 256), BF)] * 3
            + [index_rows, index_rows, pltpu.VMEM((blocks, BLOCK, 256), BF), pltpu.SemaphoreType.DMA((5 + blocks,))],
            compiler_params=PARAMS,
            cost_estimate=cost(4),
        )(edge_count, before, after, *stays(node_feat, w_qkv, w_edge, source, target, edge_feat))

    def second_part(nodes, edges):
        return pl.pallas_call(
            part_kernel,
            grid=(blocks,),
            in_specs=[SCALAR, whole(256, 256), layer_of(1, 256, 256), layer_of(1, 256, 256), ROWS, TURNED],
            out_specs=TURNED,
            out_shape=wide,
            scratch_shapes=[pltpu.VMEM((256, 512), BF)],
            compiler_params=LIGHT,
            cost_estimate=cost(2),
        )(edge_count, nodes, w_qkv, w_edge, target, edges)

    def near(nodes, before, after):
        return pl.pallas_call(
            near_kernel,
            grid=(blocks,),
            in_specs=[SCALAR, whole(256, 256), whole(2, 64, 256), whole(2, 64, 256), ROWS],
            out_specs=TURNED,
            out_shape=turned,
            scratch_shapes=[pltpu.VMEM((256, 512), BF)],
            compiler_params=LIGHT,
            cost_estimate=cost(2),
        )(edge_count, nodes, before, after, source)

    c0, c1 = pl.pallas_call(corner_kernel, out_shape=[CORNER, CORNER], compiler_params=SMALL)(*stays(node_feat, index))
    before, after = shift(c0, c1, "gx")
    low, high = turn_sides(before, after, c0, c1)
    rows, part, edges = first_part(before, after)
    nodes, c0, c1, edges = pl.pallas_call(
        first_kernel,
        grid=(blocks,),
        in_specs=layer_specs(0) + [whole(2, 2, 64)],
        out_specs=[whole(256, 256), whole(2, 64, 256), whole(2, 64, 256), TURNED],
        out_shape=[square, CORNER, CORNER, turned],
        scratch_shapes=LAYER_SCRATCH,
        compiler_params=PARAMS,
    )(edge_count, node_feat, low, high, w_qkv, gains, source, target, rows, part, edges, index)

    before, after = shift(c0, c1, "gx")
    part = second_part(nodes, edges)
    before, after, part = lax.optimization_barrier((before, after, part))
    low, high = turn_sides(before, after, c0, c1)
    rows = near(nodes, before, after)
    half = jax.ShapeDtypeStruct((64, 8, 128), F32)
    core = lax.axis_index("core")
    nodes, keep, send = pl.pallas_call(
        functools.partial(second_kernel, scale=scale),
        grid=(blocks,),
        in_specs=layer_specs(1) + [SCALAR, whole(256, 256), whole(169, 256), pl.BlockSpec((169, BLOCK), lambda i: (0, i))],
        out_specs=[whole(256, 256), whole(64, 8, 128), whole(64, 8, 128)],
        out_shape=[square, half, half],
        scratch_shapes=LAYER_SCRATCH + [
            pltpu.VMEM((256, 256), BF), pltpu.VMEM((256, 169), BF), pltpu.VMEM((256, BLOCK), BF),
            pltpu.VMEM((256, BLOCK), BF), pltpu.VMEM((256, BLOCK), BF), pltpu.VMEM((169, BLOCK), BF),
            pltpu.VMEM((256, 256), F32), pltpu.VMEM((176, 256), F32),
        ],
        compiler_params=PARAMS,
    )(
        edge_count, nodes, low, high, w_qkv, gains, source, target, rows, part, edges,
        core.astype(jnp.int32).reshape(1), head_in, head_out.T, targets,
    )
    chips = ("pair", "gx", "gy")
    parts = lax.all_to_all(keep + swap_cores(send), chips, 0, 0, tiled=True)
    share = jnp.sum(parts, axis=0)
    full = lax.all_to_all(jnp.broadcast_to(share[None], (128, 8, 128)), AXES, 0, 0, tiled=True)
    full = full.reshape(2, 2, 32, 8, 128)
    grad_in = full[:, 0].reshape(64, 8, 128)
    grad_out = full[:, 1].reshape(64, 8, 128)[0:44]
    grad_in = grad_in.reshape(32, 2, 8, 128).transpose(0, 2, 1, 3).reshape(256, 256)
    grad_out = grad_out.reshape(22, 2, 8, 128).transpose(0, 2, 1, 3).reshape(176, 256)[0:169].T
    return nodes, grad_in, grad_out


def solution(mesh):
    shape = dict(mesh.shape)
    cut = Mesh(mesh.devices.reshape(shape["rep"] // 2, 2, shape["gx"], shape["gy"]), AXES)
    tile = P(AXES)
    return jax.shard_map(
        body,
        mesh=cut,
        in_specs=(
            P(AXES, None), P(AXES, None), tile, tile, tile, P(("pair", "core"), "gx", "gy", None, None, None),
            P(), P(), P(), P(), P(), P(None, AXES),
        ),
        out_specs=(P(AXES, None), P(), P()),
        check_vma=False,
    )
```

```python
import functools

import jax
import jax.numpy as jnp
from jax import lax
from jax.experimental import pallas as pl
from jax.experimental.pallas import tpu as pltpu
from jax.sharding import Mesh
from jax.sharding import PartitionSpec as P

AXES = ("pair", "core", "gx", "gy")
BF = jnp.bfloat16
F32 = jnp.float32
BLOCK = 2048
SUB = 256
LAGS = (1, 1, 1)
VMEM_MIB = 28


def nn(a, b):
    return jnp.dot(a, b, preferred_element_type=F32)


def nt(a, b):
    return lax.dot_general(a, b, (((1,), (1,)), ((), ())), preferred_element_type=F32)


def tn(a, b):
    return lax.dot_general(a, b, (((0,), (0,)), ((), ())), preferred_element_type=F32)


def hot(row, base, rows):
    index = lax.broadcasted_iota(jnp.int16, (rows, row.shape[1]), 0)
    same = index == (row - base).astype(jnp.int16)
    return jnp.where(same, jnp.ones((), BF), jnp.zeros((), BF))


def sigmoid(x):
    return 0.5 * jnp.tanh(0.5 * x) + 0.5


def pick_corners(nodes, index_ref, c0_ref, c1_ref):
    for i, out_ref in enumerate((c0_ref, c1_ref)):
        for j in range(2):
            out_ref[j] = tn(hot(index_ref[i, j : j + 1, :], 0, 256), nodes).astype(BF)


def corner_kernel(nodes_ref, index_ref, c0_ref, c1_ref):
    pick_corners(nodes_ref[...], index_ref, c0_ref, c1_ref)


def stack_kernel(before_ref, after_ref, c0_ref, c1_ref, low_ref, high_ref):
    for j, out_ref in enumerate((low_ref, high_ref)):
        for i, cell_ref in enumerate((before_ref, c0_ref, c1_ref, after_ref)):
            out_ref[i] = cell_ref[j]


def prepare_own(nodes, wqkv, wedge, wqe_t):
    wqe_t[:, 0:256] = nn(nodes[...], wqkv[:, 0:256]).astype(BF).T
    wqe_t[:, 256:512] = wedge[...].T


def near_hot(source):
    return jnp.concatenate([hot(source, 0, 256), hot(source, 320, 128), hot(source, 832, 128)], axis=0)


def far_hot(source):
    return jnp.concatenate([hot(source, 256, 64), hot(source, 448, 384), hot(source, 960, 64)], axis=0)


def prepare_far(low_ref, high_ref, wqkv_ref, far_t, wkv_t):
    for k in range(2):
        cells = [low_ref[2 * k], high_ref[2 * k], low_ref[2 * k + 1], high_ref[2 * k + 1]]
        far_t[:, 256 * k : 256 * (k + 1)] = jnp.concatenate(cells, axis=0).T
    wkv_t[...] = wqkv_ref[:, 256:].T


def new_nodes(nodes_ref, acc, gain):
    summed = (acc[0:256, :] + acc[256:512, :]).T
    centre = summed - jnp.mean(summed, axis=-1, keepdims=True)
    spread = jnp.mean(centre * centre, axis=-1, keepdims=True)
    normed = centre * lax.rsqrt(spread + 1e-05)
    return (nodes_ref[...].astype(F32) + gain * normed).astype(BF)


def staged(stages):
    parts = BLOCK // SUB
    held = [{} for _ in range(parts)]
    lag = 0
    lags = [lag := lag + step for _, step in stages]
    for tick in range(parts + lag):
        for (stage, _), late in zip(stages, lags):
            j = tick - late
            if 0 <= j < parts:
                stage(held[j], slice(j * SUB, (j + 1) * SUB), j * SUB)


def part_of(target, edges, wqe_t):
    return nn(wqe_t[...], jnp.concatenate([hot(target, 0, 256), edges], axis=0))


def first_part_kernel(
    count_ref, nodes_hbm, wqkv_hbm, wedge_hbm, dst_hbm, edge_hbm, part_ref, turned_ref,
    wqe_t, nodes, wqkv, wedge, dst, edge, sems,
):
    step = pl.program_id(0)
    steps = edge.shape[0]
    small = [
        pltpu.make_async_copy(nodes_hbm, nodes, sems.at[0]),
        pltpu.make_async_copy(wqkv_hbm.at[0, :, pl.ds(0, 256)], wqkv, sems.at[1]),
        pltpu.make_async_copy(wedge_hbm.at[0], wedge, sems.at[2]),
        pltpu.make_async_copy(dst_hbm, dst, sems.at[3]),
    ]

    def edge_copy(i):
        return pltpu.make_async_copy(edge_hbm.at[pl.ds(i * BLOCK, BLOCK), :], edge.at[i], sems.at[4 + i])

    @pl.when(step == 0)
    def _():
        for copy in small:
            copy.start()
        for i in range(steps):
            edge_copy(i).start()
        for copy in small:
            copy.wait()
        prepare_own(nodes, wqkv, wedge, wqe_t)

    edge_copy(step).wait()

    @pl.when(step * BLOCK < count_ref[0])
    def _():
        for j in range(BLOCK // SUB):
            at = slice(j * SUB, (j + 1) * SUB)
            edges = edge[step, at, :].T
            turned_ref[0, :, at] = edges
            part_ref[0, :, at] = part_of(dst[step, :, at], edges, wqe_t)


def part_kernel(count_ref, nodes_ref, wqkv_ref, wedge_ref, dst_ref, edge_ref, part_ref, wqe_t):
    step = pl.program_id(0)

    @pl.when(step == 0)
    def _():
        prepare_own(nodes_ref, wqkv_ref, wedge_ref, wqe_t)

    @pl.when(step * BLOCK < count_ref[0])
    def _():
        for j in range(BLOCK // SUB):
            at = slice(j * SUB, (j + 1) * SUB)
            part_ref[0, :, at] = part_of(dst_ref[0, :, at], edge_ref[0, :, at], wqe_t)


def near_kernel(count_ref, nodes_ref, before_ref, after_ref, src_ref, near_ref, near_t):
    step = pl.program_id(0)

    @pl.when(step == 0)
    def _():
        near_t[:, 0:256] = nodes_ref[...].T
        cells = [before_ref[0], before_ref[1], after_ref[0], after_ref[1]]
        near_t[:, 256:512] = jnp.concatenate(cells, axis=0).T

    @pl.when(step * BLOCK < count_ref[0])
    def _():
        for j in range(BLOCK // SUB):
            at = slice(j * SUB, (j + 1) * SUB)
            near_ref[0, :, at] = nn(near_t[...], near_hot(src_ref[0, :, at])).astype(BF)


def message_stages(first, count, src_ref, dst_ref, near_ref, part_ref, edge_ref, far_t, wkv_t, hl, target_hot, keep_edges, lag):
    def gather(held, at, start):
        held["rows"] = nn(far_t[...], far_hot(src_ref[0, :, at])).astype(BF) + near_ref[0, :, at]

    def message(held, at, start):
        target = dst_ref[0, :, at]
        edges = edge_ref[0, :, at]
        kv = nn(wkv_t[...], held["rows"]).astype(BF).astype(F32)
        pre = part_ref[0, :, at] + kv[:256]
        gate = sigmoid(pre)
        held["edges"] = (edges.astype(F32) + pre * gate).astype(BF)
        keep_edges(at, held["edges"])
        weighted = gate * kv[256:]
        top = weighted.astype(BF)
        hl[0:256, at] = top
        hl[256:512, at] = (weighted - top.astype(F32)).astype(BF)
        held["live"] = first + start + lax.broadcasted_iota(jnp.int32, (1, SUB), 1) < count
        target_hot[:, at] = hot(jnp.where(held["live"], target, -1), 0, 256)

    return [(gather, 0), (message, lag)]


def first_kernel(
    count_ref, nodes_ref, low_ref, high_ref, wqkv_ref, gain_ref,
    src_ref, dst_ref, near_ref, part_ref, edge_ref, index_ref,
    out_nodes_ref, c0_ref, c1_ref, out_edge_ref,
    far_t, wkv_t, acc, hl, target_hot,
):
    step = pl.program_id(0)
    count = count_ref[0]

    @pl.when(step == 0)
    def _():
        prepare_far(low_ref, high_ref, wqkv_ref, far_t, wkv_t)
        acc[...] = jnp.zeros_like(acc)

    @pl.when(step * BLOCK < count)
    def _():
        def keep_edges(at, edges):
            out_edge_ref[0, :, at] = edges

        staged(
            message_stages(
                step * BLOCK, count, src_ref, dst_ref, near_ref, part_ref, edge_ref, far_t, wkv_t, hl, target_hot, keep_edges, 0
            )
        )
        acc[...] += nt(hl[...], target_hot[...])

    @pl.when(step == pl.num_programs(0) - 1)
    def _():
        nodes = new_nodes(nodes_ref, acc, gain_ref[0:1, :])
        out_nodes_ref[...] = nodes
        pick_corners(nodes, index_ref, c0_ref, c1_ref)


def second_kernel(
    count_ref, nodes_ref, low_ref, high_ref, wqkv_ref, gain_ref,
    src_ref, dst_ref, near_ref, part_ref, edge_ref, core_ref, hin_ref, hout_ref, goal_ref,
    out_nodes_ref, keep_ref, send_ref,
    far_t, wkv_t, acc, hl, target_hot, hin_t, hout, edges_s, dact_s, hidden_s, dpred_s, grad_in, grad_out,
    *, scale,
):
    step = pl.program_id(0)
    count = count_ref[0]

    @pl.when(step == 0)
    def _():
        prepare_far(low_ref, high_ref, wqkv_ref, far_t, wkv_t)
        hin_t[...] = hin_ref[...].T
        hout[...] = hout_ref[...].T
        acc[...] = jnp.zeros_like(acc)
        grad_in[...] = jnp.zeros_like(grad_in)
        grad_out[...] = jnp.zeros_like(grad_out)

    @pl.when(step * BLOCK < count)
    def _():
        def keep_edges(at, edges):
            edges_s[:, at] = edges

        def activate(held, at, start):
            act = nn(hin_t[...], held["edges"])
            gate = sigmoid(act)
            smooth = act * gate
            held["hidden"] = smooth.astype(BF)
            hidden_s[:, at] = held["hidden"]
            held["slope"] = gate + smooth * (1.0 - gate)

        def compare(held, at, start):
            pred = nn(hout_ref[...], held["hidden"])
            weight = jnp.where(held["live"], scale, 0.0)
            held["dpred"] = ((pred - goal_ref[:, at].astype(F32)) * weight).astype(BF)
            dpred_s[:, at] = held["dpred"]

        def back(held, at, start):
            dact_s[:, at] = (nn(hout[...], held["dpred"]) * held["slope"]).astype(BF)

        staged(
            message_stages(
                step * BLOCK, count, src_ref, dst_ref, near_ref, part_ref, edge_ref, far_t, wkv_t, hl, target_hot, keep_edges, 1
            )
            + [(activate, LAGS[0]), (compare, LAGS[1]), (back, LAGS[2])]
        )
        acc[...] += nt(hl[...], target_hot[...])
        grad_in[...] += nt(edges_s[...], dact_s[...])
        grad_out[0:169, :] += nt(dpred_s[...], hidden_s[...])

    @pl.when(step == pl.num_programs(0) - 1)
    def _():
        out_nodes_ref[...] = new_nodes(nodes_ref, acc, gain_ref[1:2, :])

        def tiles_to(total, rows, to_ref):
            for i in range(rows):
                for j in range(2):
                    to_ref[2 * i + j] = total[8 * i : 8 * i + 8, 128 * j : 128 * j + 128]
            if rows < 32:
                to_ref[2 * rows : 64] = jnp.zeros((64 - 2 * rows, 8, 128), F32)

        @pl.when(core_ref[0] == 0)
        def _():
            tiles_to(grad_in, 32, keep_ref)
            tiles_to(grad_out, 22, send_ref)

        @pl.when(core_ref[0] == 1)
        def _():
            tiles_to(grad_out, 22, keep_ref)
            tiles_to(grad_in, 32, send_ref)


def whole(*shape):
    return pl.BlockSpec(shape, lambda i: (0,) * len(shape))


def layer_of(layer, *shape):
    return pl.BlockSpec((None,) + shape, lambda i: (layer, 0, 0))


SCALAR = pl.BlockSpec(memory_space=pltpu.SMEM)
ROWS = pl.BlockSpec((1, 1, BLOCK), lambda i: (i, 0, 0))
TURNED = pl.BlockSpec((1, 256, BLOCK), lambda i: (i, 0, 0))


def layer_specs(layer):
    return [
        SCALAR, whole(256, 256), whole(4, 64, 256), whole(4, 64, 256),
        layer_of(layer, 256, 768), whole(2, 256), ROWS, ROWS, TURNED, TURNED, TURNED,
    ]


LAYER_SCRATCH = [
    pltpu.VMEM((256, 512), BF), pltpu.VMEM((512, 256), BF), pltpu.VMEM((512, 256), F32),
    pltpu.VMEM((512, BLOCK), BF), pltpu.VMEM((256, BLOCK), BF),
]
LIGHT = pltpu.CompilerParams(vmem_limit_bytes=16 * 2**20)
SMALL = pltpu.CompilerParams(vmem_limit_bytes=4 * 2**20)
PARAMS = pltpu.CompilerParams(vmem_limit_bytes=VMEM_MIB * 2**20)
CORNER = jax.ShapeDtypeStruct((2, 64, 256), BF)


def stays(*arrays):
    return [pltpu.with_memory_space_constraint(x, pltpu.HBM) for x in arrays]


def shift(low, high, axis):
    count = lax.axis_size(axis)
    up = [(i, (i + 1) % count) for i in range(count)]
    down = [(j, i) for i, j in up]
    return lax.ppermute(high, axis, up), lax.ppermute(low, axis, down)


def turn_sides(before, after, c0, c1):
    side = jax.ShapeDtypeStruct((4, 64, 256), BF)
    low, high = pl.pallas_call(stack_kernel, out_shape=[side, side], compiler_params=SMALL)(before, after, c0, c1)
    return shift(low, high, "gy")


def swap_cores(x):
    return lax.ppermute(x, "core", [(0, 1), (1, 0)])


def body(node_feat, edge_feat, edge_src, edge_dst, edge_count, send_idx, w_qkv, w_edge, gains, head_in, head_out, targets):
    slots = edge_feat.shape[0]
    blocks = slots // BLOCK
    scale = 0.125 / (slots * lax.axis_size(AXES)) ** 0.5
    core = lax.axis_index("core").astype(jnp.int32).reshape(1)
    index, core = lax.optimization_barrier((send_idx.reshape(2, 2, 64), core))
    source = edge_src.reshape(blocks, 1, BLOCK)
    target = edge_dst.reshape(blocks, 1, BLOCK)

    turned = jax.ShapeDtypeStruct((blocks, 256, BLOCK), BF)
    wide = jax.ShapeDtypeStruct((blocks, 256, BLOCK), F32)
    square = jax.ShapeDtypeStruct((256, 256), BF)

    def cost(units):
        return pl.CostEstimate(flops=2 * units * slots * 65536, bytes_accessed=units * 6 * 2**20, transcendentals=0)

    def first_part(nodes):
        stay = pl.BlockSpec(memory_space=pltpu.HBM)
        return pl.pallas_call(
            first_part_kernel,
            grid=(blocks,),
            in_specs=[SCALAR] + [stay] * 5,
            out_specs=[TURNED] * 2,
            out_shape=[wide, turned],
            scratch_shapes=[pltpu.VMEM((256, 512), BF)] + [pltpu.VMEM((256, 256), BF)] * 3
            + [
                pltpu.VMEM((blocks, 1, BLOCK), jnp.int32), pltpu.VMEM((blocks, BLOCK, 256), BF),
                pltpu.SemaphoreType.DMA((4 + blocks,)),
            ],
            compiler_params=LIGHT,
            cost_estimate=cost(2),
        )(edge_count, *stays(nodes, w_qkv, w_edge, target, edge_feat))

    def second_part(nodes, edges):
        return pl.pallas_call(
            part_kernel,
            grid=(blocks,),
            in_specs=[SCALAR, whole(256, 256), layer_of(1, 256, 256), layer_of(1, 256, 256), ROWS, TURNED],
            out_specs=TURNED,
            out_shape=wide,
            scratch_shapes=[pltpu.VMEM((256, 512), BF)],
            compiler_params=LIGHT,
            cost_estimate=cost(2),
        )(edge_count, nodes, w_qkv, w_edge, target, edges)

    def near(nodes, before, after):
        return pl.pallas_call(
            near_kernel,
            grid=(blocks,),
            in_specs=[SCALAR, whole(256, 256), whole(2, 64, 256), whole(2, 64, 256), ROWS],
            out_specs=TURNED,
            out_shape=turned,
            scratch_shapes=[pltpu.VMEM((256, 512), BF)],
            compiler_params=LIGHT,
            cost_estimate=cost(2),
        )(edge_count, nodes, before, after, source)

    c0, c1 = pl.pallas_call(corner_kernel, out_shape=[CORNER, CORNER], compiler_params=SMALL)(*stays(node_feat, index))
    before, after = shift(c0, c1, "gx")
    later_nodes, _ = lax.optimization_barrier((node_feat, c0))
    part, edges = first_part(later_nodes)
    before, after, part = lax.optimization_barrier((before, after, part))
    low, high = turn_sides(before, after, c0, c1)
    rows = near(node_feat, before, after)
    nodes, c0, c1, edges = pl.pallas_call(
        first_kernel,
        grid=(blocks,),
        in_specs=layer_specs(0) + [whole(2, 2, 64)],
        out_specs=[whole(256, 256), whole(2, 64, 256), whole(2, 64, 256), TURNED],
        out_shape=[square, CORNER, CORNER, turned],
        scratch_shapes=LAYER_SCRATCH,
        compiler_params=PARAMS,
    )(edge_count, node_feat, low, high, w_qkv, gains, source, target, rows, part, edges, index)

    before, after = shift(c0, c1, "gx")
    part = second_part(nodes, edges)
    before, after, part = lax.optimization_barrier((before, after, part))
    low, high = turn_sides(before, after, c0, c1)
    rows = near(nodes, before, after)
    half = jax.ShapeDtypeStruct((64, 8, 128), F32)
    nodes, keep, send = pl.pallas_call(
        functools.partial(second_kernel, scale=scale),
        grid=(blocks,),
        in_specs=layer_specs(1) + [SCALAR, whole(256, 256), whole(169, 256), pl.BlockSpec((169, BLOCK), lambda i: (0, i))],
        out_specs=[whole(256, 256), whole(64, 8, 128), whole(64, 8, 128)],
        out_shape=[square, half, half],
        scratch_shapes=LAYER_SCRATCH + [
            pltpu.VMEM((256, 256), BF), pltpu.VMEM((256, 169), BF), pltpu.VMEM((256, BLOCK), BF),
            pltpu.VMEM((256, BLOCK), BF), pltpu.VMEM((256, BLOCK), BF), pltpu.VMEM((169, BLOCK), BF),
            pltpu.VMEM((256, 256), F32), pltpu.VMEM((176, 256), F32),
        ],
        compiler_params=PARAMS,
    )(
        edge_count, nodes, low, high, w_qkv, gains, source, target, rows, part, edges,
        core, head_in, head_out.T, targets,
    )
    chips = ("pair", "gx", "gy")
    parts = lax.all_to_all(keep + swap_cores(send), chips, 0, 0, tiled=True)
    share = jnp.sum(parts, axis=0)
    full = lax.all_to_all(jnp.broadcast_to(share[None], (128, 8, 128)), AXES, 0, 0, tiled=True)
    full = full.reshape(2, 2, 32, 8, 128)
    grad_in = full[:, 0].reshape(64, 8, 128)
    grad_out = full[:, 1].reshape(64, 8, 128)[0:44]
    grad_in = grad_in.reshape(32, 2, 8, 128).transpose(0, 2, 1, 3).reshape(256, 256)
    grad_out = grad_out.reshape(22, 2, 8, 128).transpose(0, 2, 1, 3).reshape(176, 256)[0:169].T
    return nodes, grad_in, grad_out


def solution(mesh):
    shape = dict(mesh.shape)
    cut = Mesh(mesh.devices.reshape(shape["rep"] // 2, 2, shape["gx"], shape["gy"]), AXES)
    tile = P(AXES)
    return jax.shard_map(
        body,
        mesh=cut,
        in_specs=(
            P(AXES, None), P(AXES, None), tile, tile, tile, P(("pair", "core"), "gx", "gy", None, None, None),
            P(), P(), P(), P(), P(), P(None, AXES),
        ),
        out_specs=(P(AXES, None), P(), P()),
        check_vma=False,
    )
```

```python
import functools

import jax
import jax.numpy as jnp
from jax import lax
from jax.experimental import pallas as pl
from jax.experimental.pallas import tpu as pltpu
from jax.sharding import PartitionSpec as P

AXES = ("rep", "gx", "gy")
BF = jnp.bfloat16
F32 = jnp.float32
BLOCK = 2048
SUB = 256
LAGS = (1, 1, 1)
VMEM_MIB = 28


def nn(a, b):
    return jnp.dot(a, b, preferred_element_type=F32)


def nt(a, b):
    return lax.dot_general(a, b, (((1,), (1,)), ((), ())), preferred_element_type=F32)


def tn(a, b):
    return lax.dot_general(a, b, (((0,), (0,)), ((), ())), preferred_element_type=F32)


def hot(row, base, rows):
    index = lax.broadcasted_iota(jnp.int16, (rows, row.shape[1]), 0)
    same = index == (row - base).astype(jnp.int16)
    return jnp.where(same, jnp.ones((), BF), jnp.zeros((), BF))


def sigmoid(x):
    return 0.5 * jnp.tanh(0.5 * x) + 0.5


def pick_corners(nodes, index_ref, c0_ref, c1_ref):
    for i, out_ref in enumerate((c0_ref, c1_ref)):
        for j in range(2):
            out_ref[j] = tn(hot(index_ref[i, j : j + 1, :], 0, 256), nodes).astype(BF)


def corner_kernel(nodes_ref, index_ref, c0_ref, c1_ref):
    pick_corners(nodes_ref[...], index_ref, c0_ref, c1_ref)


def stack_kernel(before_ref, after_ref, c0_ref, c1_ref, low_ref, high_ref):
    for j, out_ref in enumerate((low_ref, high_ref)):
        for i, cell_ref in enumerate((before_ref, c0_ref, c1_ref, after_ref)):
            out_ref[i] = cell_ref[j]


def prepare_own(nodes, wqkv, wedge, wqe_t):
    wqe_t[:, 0:256] = nn(nodes[...], wqkv[:, 0:256]).astype(BF).T
    wqe_t[:, 256:512] = wedge[...].T


def near_hot(source):
    return jnp.concatenate([hot(source, 0, 256), hot(source, 320, 128), hot(source, 832, 128)], axis=0)


def far_hot(source):
    return jnp.concatenate([hot(source, 256, 64), hot(source, 448, 384), hot(source, 960, 64)], axis=0)


def prepare_far(low_ref, high_ref, wqkv_ref, far_t, wkv_t):
    for k in range(2):
        cells = [low_ref[2 * k], high_ref[2 * k], low_ref[2 * k + 1], high_ref[2 * k + 1]]
        far_t[:, 256 * k : 256 * (k + 1)] = jnp.concatenate(cells, axis=0).T
    wkv_t[...] = wqkv_ref[:, 256:].T


def new_nodes(nodes_ref, acc, gain):
    summed = (acc[0:256, :] + acc[256:512, :]).T
    centre = summed - jnp.mean(summed, axis=-1, keepdims=True)
    spread = jnp.mean(centre * centre, axis=-1, keepdims=True)
    normed = centre * lax.rsqrt(spread + 1e-05)
    return (nodes_ref[...].astype(F32) + gain * normed).astype(BF)


def staged(stages):
    parts = BLOCK // SUB
    held = [{} for _ in range(parts)]
    lag = 0
    lags = [lag := lag + step for _, step in stages]
    for tick in range(parts + lag):
        for (stage, _), late in zip(stages, lags):
            j = tick - late
            if 0 <= j < parts:
                stage(held[j], slice(j * SUB, (j + 1) * SUB), j * SUB)


def part_of(target, edges, wqe_t):
    return nn(wqe_t[...], jnp.concatenate([hot(target, 0, 256), edges], axis=0))


def first_part_kernel(
    count_ref, nodes_hbm, wqkv_hbm, wedge_hbm, dst_hbm, edge_hbm, part_ref, turned_ref,
    wqe_t, nodes, wqkv, wedge, dst, edge, sems,
):
    step = pl.program_id(0)
    steps = edge.shape[0]
    small = [
        pltpu.make_async_copy(nodes_hbm, nodes, sems.at[0]),
        pltpu.make_async_copy(wqkv_hbm.at[0, :, pl.ds(0, 256)], wqkv, sems.at[1]),
        pltpu.make_async_copy(wedge_hbm.at[0], wedge, sems.at[2]),
        pltpu.make_async_copy(dst_hbm, dst, sems.at[3]),
    ]

    def edge_copy(i):
        return pltpu.make_async_copy(edge_hbm.at[pl.ds(i * BLOCK, BLOCK), :], edge.at[i], sems.at[4 + i])

    @pl.when(step == 0)
    def _():
        for copy in small:
            copy.start()
        for i in range(steps):
            edge_copy(i).start()
        for copy in small:
            copy.wait()
        prepare_own(nodes, wqkv, wedge, wqe_t)

    edge_copy(step).wait()

    @pl.when(step * BLOCK < count_ref[0])
    def _():
        for j in range(BLOCK // SUB):
            at = slice(j * SUB, (j + 1) * SUB)
            edges = edge[step, at, :].T
            turned_ref[0, :, at] = edges
            part_ref[0, :, at] = part_of(dst[step, :, at], edges, wqe_t)


def part_kernel(count_ref, nodes_ref, wqkv_ref, wedge_ref, dst_ref, edge_ref, part_ref, wqe_t):
    step = pl.program_id(0)

    @pl.when(step == 0)
    def _():
        prepare_own(nodes_ref, wqkv_ref, wedge_ref, wqe_t)

    @pl.when(step * BLOCK < count_ref[0])
    def _():
        for j in range(BLOCK // SUB):
            at = slice(j * SUB, (j + 1) * SUB)
            part_ref[0, :, at] = part_of(dst_ref[0, :, at], edge_ref[0, :, at], wqe_t)


def near_kernel(count_ref, nodes_ref, before_ref, after_ref, src_ref, near_ref, near_t):
    step = pl.program_id(0)

    @pl.when(step == 0)
    def _():
        near_t[:, 0:256] = nodes_ref[...].T
        cells = [before_ref[0], before_ref[1], after_ref[0], after_ref[1]]
        near_t[:, 256:512] = jnp.concatenate(cells, axis=0).T

    @pl.when(step * BLOCK < count_ref[0])
    def _():
        for j in range(BLOCK // SUB):
            at = slice(j * SUB, (j + 1) * SUB)
            near_ref[0, :, at] = nn(near_t[...], near_hot(src_ref[0, :, at])).astype(BF)


def message_stages(first, count, src_ref, dst_ref, near_ref, part_ref, edge_ref, far_t, wkv_t, hl, target_hot, keep_edges, lag):
    def gather(held, at, start):
        held["rows"] = nn(far_t[...], far_hot(src_ref[0, :, at])).astype(BF) + near_ref[0, :, at]

    def message(held, at, start):
        target = dst_ref[0, :, at]
        edges = edge_ref[0, :, at]
        kv = nn(wkv_t[...], held["rows"]).astype(BF).astype(F32)
        pre = part_ref[0, :, at] + kv[:256]
        gate = sigmoid(pre)
        held["edges"] = (edges.astype(F32) + pre * gate).astype(BF)
        keep_edges(at, held["edges"])
        weighted = gate * kv[256:]
        top = weighted.astype(BF)
        hl[0:256, at] = top
        hl[256:512, at] = (weighted - top.astype(F32)).astype(BF)
        held["live"] = first + start + lax.broadcasted_iota(jnp.int32, (1, SUB), 1) < count
        target_hot[:, at] = hot(jnp.where(held["live"], target, -1), 0, 256)

    return [(gather, 0), (message, lag)]


def first_kernel(
    count_ref, nodes_ref, low_ref, high_ref, wqkv_ref, gain_ref,
    src_ref, dst_ref, near_ref, part_ref, edge_ref, index_ref,
    out_nodes_ref, c0_ref, c1_ref, out_edge_ref,
    far_t, wkv_t, acc, hl, target_hot,
):
    step = pl.program_id(0)
    count = count_ref[0]

    @pl.when(step == 0)
    def _():
        prepare_far(low_ref, high_ref, wqkv_ref, far_t, wkv_t)
        acc[...] = jnp.zeros_like(acc)

    @pl.when(step * BLOCK < count)
    def _():
        def keep_edges(at, edges):
            out_edge_ref[0, :, at] = edges

        staged(
            message_stages(
                step * BLOCK, count, src_ref, dst_ref, near_ref, part_ref, edge_ref, far_t, wkv_t, hl, target_hot, keep_edges, 0
            )
        )
        acc[...] += nt(hl[...], target_hot[...])

    @pl.when(step == pl.num_programs(0) - 1)
    def _():
        nodes = new_nodes(nodes_ref, acc, gain_ref[0:1, :])
        out_nodes_ref[...] = nodes
        pick_corners(nodes, index_ref, c0_ref, c1_ref)


def second_kernel(
    count_ref, nodes_ref, low_ref, high_ref, wqkv_ref, gain_ref,
    src_ref, dst_ref, near_ref, part_ref, edge_ref, hin_ref, hout_ref, goal_ref,
    out_nodes_ref, grad_ref,
    far_t, wkv_t, acc, hl, target_hot, hin_t, hout, edges_s, dact_s, hidden_s, dpred_s, grad_in, grad_out,
    *, scale,
):
    step = pl.program_id(0)
    count = count_ref[0]

    @pl.when(step == 0)
    def _():
        prepare_far(low_ref, high_ref, wqkv_ref, far_t, wkv_t)
        hin_t[...] = hin_ref[...].T
        hout[...] = hout_ref[...].T
        acc[...] = jnp.zeros_like(acc)
        grad_in[...] = jnp.zeros_like(grad_in)
        grad_out[...] = jnp.zeros_like(grad_out)

    @pl.when(step * BLOCK < count)
    def _():
        def keep_edges(at, edges):
            edges_s[:, at] = edges

        def activate(held, at, start):
            act = nn(hin_t[...], held["edges"])
            gate = sigmoid(act)
            smooth = act * gate
            held["hidden"] = smooth.astype(BF)
            hidden_s[:, at] = held["hidden"]
            held["slope"] = gate + smooth * (1.0 - gate)

        def compare(held, at, start):
            pred = nn(hout_ref[...], held["hidden"])
            weight = jnp.where(held["live"], scale, 0.0)
            held["dpred"] = ((pred - goal_ref[:, at].astype(F32)) * weight).astype(BF)
            dpred_s[:, at] = held["dpred"]

        def back(held, at, start):
            dact_s[:, at] = (nn(hout[...], held["dpred"]) * held["slope"]).astype(BF)

        staged(
            message_stages(
                step * BLOCK, count, src_ref, dst_ref, near_ref, part_ref, edge_ref, far_t, wkv_t, hl, target_hot, keep_edges, 1
            )
            + [(activate, LAGS[0]), (compare, LAGS[1]), (back, LAGS[2])]
        )
        acc[...] += nt(hl[...], target_hot[...])
        grad_in[...] += nt(edges_s[...], dact_s[...])
        grad_out[0:169, :] += nt(dpred_s[...], hidden_s[...])

    @pl.when(step == pl.num_programs(0) - 1)
    def _():
        out_nodes_ref[...] = new_nodes(nodes_ref, acc, gain_ref[1:2, :])
        tile = 0
        for total, rows in ((grad_in, 32), (grad_out, 22)):
            for i in range(rows):
                for j in range(2):
                    grad_ref[tile] = total[8 * i : 8 * i + 8, 128 * j : 128 * j + 128]
                    tile += 1
        grad_ref[tile:128] = jnp.zeros((128 - tile, 8, 128), F32)


def whole(*shape):
    return pl.BlockSpec(shape, lambda i: (0,) * len(shape))


def layer_of(layer, *shape):
    return pl.BlockSpec((None,) + shape, lambda i: (layer, 0, 0))


SCALAR = pl.BlockSpec(memory_space=pltpu.SMEM)
ROWS = pl.BlockSpec((1, 1, BLOCK), lambda i: (i, 0, 0))
TURNED = pl.BlockSpec((1, 256, BLOCK), lambda i: (i, 0, 0))


def layer_specs(layer):
    return [
        SCALAR, whole(256, 256), whole(4, 64, 256), whole(4, 64, 256),
        layer_of(layer, 256, 768), whole(2, 256), ROWS, ROWS, TURNED, TURNED, TURNED,
    ]


LAYER_SCRATCH = [
    pltpu.VMEM((256, 512), BF), pltpu.VMEM((512, 256), BF), pltpu.VMEM((512, 256), F32),
    pltpu.VMEM((512, BLOCK), BF), pltpu.VMEM((256, BLOCK), BF),
]
LIGHT = pltpu.CompilerParams(vmem_limit_bytes=16 * 2**20)
SMALL = pltpu.CompilerParams(vmem_limit_bytes=4 * 2**20)
PARAMS = pltpu.CompilerParams(vmem_limit_bytes=VMEM_MIB * 2**20)
CORNER = jax.ShapeDtypeStruct((2, 64, 256), BF)


def stays(*arrays):
    return [pltpu.with_memory_space_constraint(x, pltpu.HBM) for x in arrays]


def shift(low, high, axis):
    count = lax.axis_size(axis)
    up = [(i, (i + 1) % count) for i in range(count)]
    down = [(j, i) for i, j in up]
    return lax.ppermute(high, axis, up), lax.ppermute(low, axis, down)


def turn_sides(before, after, c0, c1):
    side = jax.ShapeDtypeStruct((4, 64, 256), BF)
    low, high = pl.pallas_call(stack_kernel, out_shape=[side, side], compiler_params=SMALL)(before, after, c0, c1)
    return shift(low, high, "gy")


def body(node_feat, edge_feat, edge_src, edge_dst, edge_count, send_idx, w_qkv, w_edge, gains, head_in, head_out, targets):
    slots = edge_feat.shape[0]
    blocks = slots // BLOCK
    scale = 0.125 / (slots * lax.axis_size(AXES)) ** 0.5
    index = send_idx.reshape(2, 2, 64)
    source = edge_src.reshape(blocks, 1, BLOCK)
    target = edge_dst.reshape(blocks, 1, BLOCK)

    turned = jax.ShapeDtypeStruct((blocks, 256, BLOCK), BF)
    wide = jax.ShapeDtypeStruct((blocks, 256, BLOCK), F32)
    square = jax.ShapeDtypeStruct((256, 256), BF)

    def cost(units):
        return pl.CostEstimate(flops=2 * units * slots * 65536, bytes_accessed=units * 6 * 2**20, transcendentals=0)

    def first_part(nodes):
        stay = pl.BlockSpec(memory_space=pltpu.HBM)
        return pl.pallas_call(
            first_part_kernel,
            grid=(blocks,),
            in_specs=[SCALAR] + [stay] * 5,
            out_specs=[TURNED] * 2,
            out_shape=[wide, turned],
            scratch_shapes=[pltpu.VMEM((256, 512), BF)] + [pltpu.VMEM((256, 256), BF)] * 3
            + [
                pltpu.VMEM((blocks, 1, BLOCK), jnp.int32), pltpu.VMEM((blocks, BLOCK, 256), BF),
                pltpu.SemaphoreType.DMA((4 + blocks,)),
            ],
            compiler_params=LIGHT,
            cost_estimate=cost(2),
        )(edge_count, *stays(nodes, w_qkv, w_edge, target, edge_feat))

    def second_part(nodes, edges):
        return pl.pallas_call(
            part_kernel,
            grid=(blocks,),
            in_specs=[SCALAR, whole(256, 256), layer_of(1, 256, 256), layer_of(1, 256, 256), ROWS, TURNED],
            out_specs=TURNED,
            out_shape=wide,
            scratch_shapes=[pltpu.VMEM((256, 512), BF)],
            compiler_params=LIGHT,
            cost_estimate=cost(2),
        )(edge_count, nodes, w_qkv, w_edge, target, edges)

    def near(nodes, before, after):
        return pl.pallas_call(
            near_kernel,
            grid=(blocks,),
            in_specs=[SCALAR, whole(256, 256), whole(2, 64, 256), whole(2, 64, 256), ROWS],
            out_specs=TURNED,
            out_shape=turned,
            scratch_shapes=[pltpu.VMEM((256, 512), BF)],
            compiler_params=LIGHT,
            cost_estimate=cost(2),
        )(edge_count, nodes, before, after, source)

    c0, c1 = pl.pallas_call(corner_kernel, out_shape=[CORNER, CORNER], compiler_params=SMALL)(*stays(node_feat, index))
    before, after = shift(c0, c1, "gx")
    later_nodes, _ = lax.optimization_barrier((node_feat, c0))
    part, edges = first_part(later_nodes)
    before, after, part = lax.optimization_barrier((before, after, part))
    low, high = turn_sides(before, after, c0, c1)
    rows = near(node_feat, before, after)
    nodes, c0, c1, edges = pl.pallas_call(
        first_kernel,
        grid=(blocks,),
        in_specs=layer_specs(0) + [whole(2, 2, 64)],
        out_specs=[whole(256, 256), whole(2, 64, 256), whole(2, 64, 256), TURNED],
        out_shape=[square, CORNER, CORNER, turned],
        scratch_shapes=LAYER_SCRATCH,
        compiler_params=PARAMS,
    )(edge_count, node_feat, low, high, w_qkv, gains, source, target, rows, part, edges, index)

    before, after = shift(c0, c1, "gx")
    part = second_part(nodes, edges)
    before, after, part = lax.optimization_barrier((before, after, part))
    low, high = turn_sides(before, after, c0, c1)
    rows = near(nodes, before, after)
    nodes, grads = pl.pallas_call(
        functools.partial(second_kernel, scale=scale),
        grid=(blocks,),
        in_specs=layer_specs(1) + [whole(256, 256), whole(169, 256), pl.BlockSpec((169, BLOCK), lambda i: (0, i))],
        out_specs=[whole(256, 256), whole(128, 8, 128)],
        out_shape=[square, jax.ShapeDtypeStruct((128, 8, 128), F32)],
        scratch_shapes=LAYER_SCRATCH + [
            pltpu.VMEM((256, 256), BF), pltpu.VMEM((256, 169), BF), pltpu.VMEM((256, BLOCK), BF),
            pltpu.VMEM((256, BLOCK), BF), pltpu.VMEM((256, BLOCK), BF), pltpu.VMEM((169, BLOCK), BF),
            pltpu.VMEM((256, 256), F32), pltpu.VMEM((176, 256), F32),
        ],
        compiler_params=PARAMS,
    )(
        edge_count, nodes, low, high, w_qkv, gains, source, target, rows, part, edges,
        head_in, head_out.T, targets,
    )
    parts = lax.all_to_all(grads, AXES, 0, 0, tiled=True)
    share = jnp.sum(parts, axis=0)
    full = lax.all_to_all(jnp.broadcast_to(share[None], (128, 8, 128)), AXES, 0, 0, tiled=True)
    grad_in = full[0:64].reshape(32, 2, 8, 128).transpose(0, 2, 1, 3).reshape(256, 256)
    grad_out = full[64:108].reshape(22, 2, 8, 128).transpose(0, 2, 1, 3).reshape(176, 256)[0:169].T
    return nodes, grad_in, grad_out


def solution(mesh):
    tile = P(AXES)
    return jax.shard_map(
        body,
        mesh=mesh,
        in_specs=(
            P(AXES, None), P(AXES, None), tile, tile, tile, P("rep", "gx", "gy", None, None, None),
            P(), P(), P(), P(), P(), P(None, AXES),
        ),
        out_specs=(P(AXES, None), P(), P()),
        check_vma=False,
    )
```

```python
import functools

import jax
import jax.numpy as jnp
from jax import lax
from jax.experimental import pallas as pl
from jax.experimental.pallas import tpu as pltpu
from jax.sharding import Mesh
from jax.sharding import PartitionSpec as P

AXES = ("pair", "core", "gx", "gy")
BF = jnp.bfloat16
F32 = jnp.float32
BLOCK = 2048
SUB = 256
LAGS = (1, 1, 1)
VMEM_MIB = 28


def nn(a, b):
    return jnp.dot(a, b, preferred_element_type=F32)


def nt(a, b):
    return lax.dot_general(a, b, (((1,), (1,)), ((), ())), preferred_element_type=F32)


def tn(a, b):
    return lax.dot_general(a, b, (((0,), (0,)), ((), ())), preferred_element_type=F32)


def hot(row, base, rows):
    index = lax.broadcasted_iota(jnp.int16, (rows, row.shape[1]), 0)
    same = index == (row - base).astype(jnp.int16)
    return jnp.where(same, jnp.ones((), BF), jnp.zeros((), BF))


def sigmoid(x):
    return 0.5 * jnp.tanh(0.5 * x) + 0.5


def pick_corners(nodes, index_ref, c0_ref, c1_ref):
    for i, out_ref in enumerate((c0_ref, c1_ref)):
        for j in range(2):
            out_ref[j] = tn(hot(index_ref[i, j : j + 1, :], 0, 256), nodes).astype(BF)


def corner_kernel(nodes_ref, index_ref, c0_ref, c1_ref):
    pick_corners(nodes_ref[...], index_ref, c0_ref, c1_ref)


def stack_kernel(before_ref, after_ref, c0_ref, c1_ref, low_ref, high_ref):
    for j, out_ref in enumerate((low_ref, high_ref)):
        for i, cell_ref in enumerate((before_ref, c0_ref, c1_ref, after_ref)):
            out_ref[i] = cell_ref[j]


def prepare_own(nodes, wqkv, wedge, wqe_t):
    wqe_t[:, 0:256] = nn(nodes[...], wqkv[:, 0:256]).astype(BF).T
    wqe_t[:, 256:512] = wedge[...].T


def near_hot(source):
    return jnp.concatenate([hot(source, 0, 256), hot(source, 320, 128), hot(source, 832, 128)], axis=0)


def far_hot(source):
    return jnp.concatenate([hot(source, 256, 64), hot(source, 448, 384), hot(source, 960, 64)], axis=0)


def prepare_far(low_ref, high_ref, wqkv_ref, far_t, wkv_t):
    for k in range(2):
        cells = [low_ref[2 * k], high_ref[2 * k], low_ref[2 * k + 1], high_ref[2 * k + 1]]
        far_t[:, 256 * k : 256 * (k + 1)] = jnp.concatenate(cells, axis=0).T
    wkv_t[...] = wqkv_ref[:, 256:].T


def new_nodes(nodes_ref, acc, gain):
    summed = (acc[0:256, :] + acc[256:512, :]).T
    centre = summed - jnp.mean(summed, axis=-1, keepdims=True)
    spread = jnp.mean(centre * centre, axis=-1, keepdims=True)
    normed = centre * lax.rsqrt(spread + 1e-05)
    return (nodes_ref[...].astype(F32) + gain * normed).astype(BF)


def staged(stages):
    parts = BLOCK // SUB
    held = [{} for _ in range(parts)]
    lag = 0
    lags = [lag := lag + step for _, step in stages]
    for tick in range(parts + lag):
        for (stage, _), late in zip(stages, lags):
            j = tick - late
            if 0 <= j < parts:
                stage(held[j], slice(j * SUB, (j + 1) * SUB), j * SUB)


def part_of(target, edges, wqe_t):
    return nn(wqe_t[...], jnp.concatenate([hot(target, 0, 256), edges], axis=0))


def first_part_kernel(
    count_ref, nodes_hbm, wqkv_hbm, wedge_hbm, dst_hbm, edge_hbm, part_ref, turned_ref,
    wqe_t, nodes, wqkv, wedge, dst, edge, sems,
):
    step = pl.program_id(0)
    steps = edge.shape[0]
    small = [
        pltpu.make_async_copy(nodes_hbm, nodes, sems.at[0]),
        pltpu.make_async_copy(wqkv_hbm.at[0, :, pl.ds(0, 256)], wqkv, sems.at[1]),
        pltpu.make_async_copy(wedge_hbm.at[0], wedge, sems.at[2]),
        pltpu.make_async_copy(dst_hbm, dst, sems.at[3]),
    ]

    def edge_copy(i):
        return pltpu.make_async_copy(edge_hbm.at[pl.ds(i * BLOCK, BLOCK), :], edge.at[i], sems.at[4 + i])

    @pl.when(step == 0)
    def _():
        for copy in small:
            copy.start()
        for i in range(steps):
            edge_copy(i).start()
        for copy in small:
            copy.wait()
        prepare_own(nodes, wqkv, wedge, wqe_t)

    edge_copy(step).wait()

    @pl.when(step * BLOCK < count_ref[0])
    def _():
        for j in range(BLOCK // SUB):
            at = slice(j * SUB, (j + 1) * SUB)
            edges = edge[step, at, :].T
            turned_ref[0, :, at] = edges
            part_ref[0, :, at] = part_of(dst[step, :, at], edges, wqe_t)


def part_kernel(count_ref, nodes_ref, wqkv_ref, wedge_ref, dst_ref, edge_ref, part_ref, wqe_t):
    step = pl.program_id(0)

    @pl.when(step == 0)
    def _():
        prepare_own(nodes_ref, wqkv_ref, wedge_ref, wqe_t)

    @pl.when(step * BLOCK < count_ref[0])
    def _():
        for j in range(BLOCK // SUB):
            at = slice(j * SUB, (j + 1) * SUB)
            part_ref[0, :, at] = part_of(dst_ref[0, :, at], edge_ref[0, :, at], wqe_t)


def near_kernel(count_ref, nodes_ref, before_ref, after_ref, src_ref, near_ref, near_t):
    step = pl.program_id(0)

    @pl.when(step == 0)
    def _():
        near_t[:, 0:256] = nodes_ref[...].T
        cells = [before_ref[0], before_ref[1], after_ref[0], after_ref[1]]
        near_t[:, 256:512] = jnp.concatenate(cells, axis=0).T

    @pl.when(step * BLOCK < count_ref[0])
    def _():
        for j in range(BLOCK // SUB):
            at = slice(j * SUB, (j + 1) * SUB)
            near_ref[0, :, at] = nn(near_t[...], near_hot(src_ref[0, :, at])).astype(BF)


def message_stages(first, count, src_ref, dst_ref, near_ref, part_ref, edge_ref, far_t, wkv_t, hl, target_hot, keep_edges, lag):
    def gather(held, at, start):
        held["rows"] = nn(far_t[...], far_hot(src_ref[0, :, at])).astype(BF) + near_ref[0, :, at]

    def message(held, at, start):
        target = dst_ref[0, :, at]
        edges = edge_ref[0, :, at]
        kv = nn(wkv_t[...], held["rows"]).astype(BF).astype(F32)
        pre = part_ref[0, :, at] + kv[:256]
        gate = sigmoid(pre)
        held["edges"] = (edges.astype(F32) + pre * gate).astype(BF)
        keep_edges(at, held["edges"])
        weighted = gate * kv[256:]
        top = weighted.astype(BF)
        hl[0:256, at] = top
        hl[256:512, at] = (weighted - top.astype(F32)).astype(BF)
        held["live"] = first + start + lax.broadcasted_iota(jnp.int32, (1, SUB), 1) < count
        target_hot[:, at] = hot(jnp.where(held["live"], target, -1), 0, 256)

    return [(gather, 0), (message, lag)]


def first_kernel(
    count_ref, nodes_ref, low_ref, high_ref, wqkv_ref, gain_ref,
    src_ref, dst_ref, near_ref, part_ref, edge_ref, index_ref,
    out_nodes_ref, c0_ref, c1_ref, out_edge_ref,
    far_t, wkv_t, acc, hl, target_hot,
):
    step = pl.program_id(0)
    count = count_ref[0]

    @pl.when(step == 0)
    def _():
        prepare_far(low_ref, high_ref, wqkv_ref, far_t, wkv_t)
        acc[...] = jnp.zeros_like(acc)

    @pl.when(step * BLOCK < count)
    def _():
        def keep_edges(at, edges):
            out_edge_ref[0, :, at] = edges

        staged(
            message_stages(
                step * BLOCK, count, src_ref, dst_ref, near_ref, part_ref, edge_ref, far_t, wkv_t, hl, target_hot, keep_edges, 0
            )
        )
        acc[...] += nt(hl[...], target_hot[...])

    @pl.when(step == pl.num_programs(0) - 1)
    def _():
        nodes = new_nodes(nodes_ref, acc, gain_ref[0:1, :])
        out_nodes_ref[...] = nodes
        pick_corners(nodes, index_ref, c0_ref, c1_ref)


def second_kernel(
    count_ref, nodes_ref, low_ref, high_ref, wqkv_ref, gain_ref,
    src_ref, dst_ref, near_ref, part_ref, edge_ref, core_ref, hin_ref, hout_ref, goal_ref,
    acc_ref, keep_ref, send_ref,
    far_t, wkv_t, acc, hl, target_hot, hin_t, hout, edges_s, dact_s, hidden_s, dpred_s, grad_in, grad_out,
    *, scale,
):
    step = pl.program_id(0)
    count = count_ref[0]

    @pl.when(step == 0)
    def _():
        prepare_far(low_ref, high_ref, wqkv_ref, far_t, wkv_t)
        hin_t[...] = hin_ref[...].T
        hout[...] = hout_ref[...].T
        acc[...] = jnp.zeros_like(acc)
        grad_in[...] = jnp.zeros_like(grad_in)
        grad_out[...] = jnp.zeros_like(grad_out)

    @pl.when(step * BLOCK < count)
    def _():
        def keep_edges(at, edges):
            edges_s[:, at] = edges

        def activate(held, at, start):
            act = nn(hin_t[...], held["edges"])
            gate = sigmoid(act)
            smooth = act * gate
            held["hidden"] = smooth.astype(BF)
            hidden_s[:, at] = held["hidden"]
            held["slope"] = gate + smooth * (1.0 - gate)

        def compare(held, at, start):
            pred = nn(hout_ref[...], held["hidden"])
            weight = jnp.where(held["live"], scale, 0.0)
            held["dpred"] = ((pred - goal_ref[:, at].astype(F32)) * weight).astype(BF)
            dpred_s[:, at] = held["dpred"]

        def back(held, at, start):
            dact_s[:, at] = (nn(hout[...], held["dpred"]) * held["slope"]).astype(BF)

        staged(
            message_stages(
                step * BLOCK, count, src_ref, dst_ref, near_ref, part_ref, edge_ref, far_t, wkv_t, hl, target_hot, keep_edges, 1
            )
            + [(activate, LAGS[0]), (compare, LAGS[1]), (back, LAGS[2])]
        )
        acc[...] += nt(hl[...], target_hot[...])
        grad_in[...] += nt(edges_s[...], dact_s[...])
        grad_out[0:169, :] += nt(dpred_s[...], hidden_s[...])

    @pl.when(step == pl.num_programs(0) - 1)
    def _():
        acc_ref[...] = acc[...]

        def tiles_to(total, rows, to_ref):
            for i in range(rows):
                for j in range(2):
                    to_ref[2 * i + j] = total[8 * i : 8 * i + 8, 128 * j : 128 * j + 128]
            if rows < 32:
                to_ref[2 * rows : 64] = jnp.zeros((64 - 2 * rows, 8, 128), F32)

        @pl.when(core_ref[0] == 0)
        def _():
            tiles_to(grad_in, 32, keep_ref)
            tiles_to(grad_out, 22, send_ref)

        @pl.when(core_ref[0] == 1)
        def _():
            tiles_to(grad_out, 22, keep_ref)
            tiles_to(grad_in, 32, send_ref)


def update_kernel(nodes_ref, acc_ref, gain_ref, out_nodes_ref):
    out_nodes_ref[...] = new_nodes(nodes_ref, acc_ref, gain_ref[1:2, :])


def whole(*shape):
    return pl.BlockSpec(shape, lambda i: (0,) * len(shape))


def layer_of(layer, *shape):
    return pl.BlockSpec((None,) + shape, lambda i: (layer, 0, 0))


SCALAR = pl.BlockSpec(memory_space=pltpu.SMEM)
ROWS = pl.BlockSpec((1, 1, BLOCK), lambda i: (i, 0, 0))
TURNED = pl.BlockSpec((1, 256, BLOCK), lambda i: (i, 0, 0))


def layer_specs(layer):
    return [
        SCALAR, whole(256, 256), whole(4, 64, 256), whole(4, 64, 256),
        layer_of(layer, 256, 768), whole(2, 256), ROWS, ROWS, TURNED, TURNED, TURNED,
    ]


LAYER_SCRATCH = [
    pltpu.VMEM((256, 512), BF), pltpu.VMEM((512, 256), BF), pltpu.VMEM((512, 256), F32),
    pltpu.VMEM((512, BLOCK), BF), pltpu.VMEM((256, BLOCK), BF),
]
LIGHT = pltpu.CompilerParams(vmem_limit_bytes=16 * 2**20)
SMALL = pltpu.CompilerParams(vmem_limit_bytes=4 * 2**20)
PARAMS = pltpu.CompilerParams(vmem_limit_bytes=VMEM_MIB * 2**20)
CORNER = jax.ShapeDtypeStruct((2, 64, 256), BF)


def stays(*arrays):
    return [pltpu.with_memory_space_constraint(x, pltpu.HBM) for x in arrays]


def shift(low, high, axis):
    count = lax.axis_size(axis)
    up = [(i, (i + 1) % count) for i in range(count)]
    down = [(j, i) for i, j in up]
    return lax.ppermute(high, axis, up), lax.ppermute(low, axis, down)


def turn_sides(before, after, c0, c1):
    side = jax.ShapeDtypeStruct((4, 64, 256), BF)
    low, high = pl.pallas_call(stack_kernel, out_shape=[side, side], compiler_params=SMALL)(before, after, c0, c1)
    return shift(low, high, "gy")


def swap_cores(x):
    return lax.ppermute(x, "core", [(0, 1), (1, 0)])


def body(node_feat, edge_feat, edge_src, edge_dst, edge_count, send_idx, w_qkv, w_edge, gains, head_in, head_out, targets):
    slots = edge_feat.shape[0]
    blocks = slots // BLOCK
    scale = 0.125 / (slots * lax.axis_size(AXES)) ** 0.5
    core = lax.axis_index("core").astype(jnp.int32).reshape(1)
    index, core = lax.optimization_barrier((send_idx.reshape(2, 2, 64), core))
    source = edge_src.reshape(blocks, 1, BLOCK)
    target = edge_dst.reshape(blocks, 1, BLOCK)

    turned = jax.ShapeDtypeStruct((blocks, 256, BLOCK), BF)
    wide = jax.ShapeDtypeStruct((blocks, 256, BLOCK), F32)
    square = jax.ShapeDtypeStruct((256, 256), BF)

    def cost(units):
        return pl.CostEstimate(flops=2 * units * slots * 65536, bytes_accessed=units * 6 * 2**20, transcendentals=0)

    def first_part(nodes):
        stay = pl.BlockSpec(memory_space=pltpu.HBM)
        return pl.pallas_call(
            first_part_kernel,
            grid=(blocks,),
            in_specs=[SCALAR] + [stay] * 5,
            out_specs=[TURNED] * 2,
            out_shape=[wide, turned],
            scratch_shapes=[pltpu.VMEM((256, 512), BF)] + [pltpu.VMEM((256, 256), BF)] * 3
            + [
                pltpu.VMEM((blocks, 1, BLOCK), jnp.int32), pltpu.VMEM((blocks, BLOCK, 256), BF),
                pltpu.SemaphoreType.DMA((4 + blocks,)),
            ],
            compiler_params=LIGHT,
            cost_estimate=cost(2),
        )(edge_count, *stays(nodes, w_qkv, w_edge, target, edge_feat))

    def second_part(nodes, edges):
        return pl.pallas_call(
            part_kernel,
            grid=(blocks,),
            in_specs=[SCALAR, whole(256, 256), layer_of(1, 256, 256), layer_of(1, 256, 256), ROWS, TURNED],
            out_specs=TURNED,
            out_shape=wide,
            scratch_shapes=[pltpu.VMEM((256, 512), BF)],
            compiler_params=LIGHT,
            cost_estimate=cost(2),
        )(edge_count, nodes, w_qkv, w_edge, target, edges)

    def near(nodes, before, after):
        return pl.pallas_call(
            near_kernel,
            grid=(blocks,),
            in_specs=[SCALAR, whole(256, 256), whole(2, 64, 256), whole(2, 64, 256), ROWS],
            out_specs=TURNED,
            out_shape=turned,
            scratch_shapes=[pltpu.VMEM((256, 512), BF)],
            compiler_params=LIGHT,
            cost_estimate=cost(2),
        )(edge_count, nodes, before, after, source)

    c0, c1 = pl.pallas_call(corner_kernel, out_shape=[CORNER, CORNER], compiler_params=SMALL)(*stays(node_feat, index))
    before, after = shift(c0, c1, "gx")
    later_nodes, _ = lax.optimization_barrier((node_feat, c0))
    part, edges = first_part(later_nodes)
    before, after, part = lax.optimization_barrier((before, after, part))
    low, high = turn_sides(before, after, c0, c1)
    rows = near(node_feat, before, after)
    nodes, c0, c1, edges = pl.pallas_call(
        first_kernel,
        grid=(blocks,),
        in_specs=layer_specs(0) + [whole(2, 2, 64)],
        out_specs=[whole(256, 256), whole(2, 64, 256), whole(2, 64, 256), TURNED],
        out_shape=[square, CORNER, CORNER, turned],
        scratch_shapes=LAYER_SCRATCH,
        compiler_params=PARAMS,
    )(edge_count, node_feat, low, high, w_qkv, gains, source, target, rows, part, edges, index)

    before, after = shift(c0, c1, "gx")
    part = second_part(nodes, edges)
    before, after, part = lax.optimization_barrier((before, after, part))
    low, high = turn_sides(before, after, c0, c1)
    rows = near(nodes, before, after)
    half = jax.ShapeDtypeStruct((64, 8, 128), F32)
    acc, keep, send = pl.pallas_call(
        functools.partial(second_kernel, scale=scale),
        grid=(blocks,),
        in_specs=layer_specs(1) + [SCALAR, whole(256, 256), whole(169, 256), pl.BlockSpec((169, BLOCK), lambda i: (0, i))],
        out_specs=[whole(512, 256), whole(64, 8, 128), whole(64, 8, 128)],
        out_shape=[jax.ShapeDtypeStruct((512, 256), F32), half, half],
        scratch_shapes=LAYER_SCRATCH + [
            pltpu.VMEM((256, 256), BF), pltpu.VMEM((256, 169), BF), pltpu.VMEM((256, BLOCK), BF),
            pltpu.VMEM((256, BLOCK), BF), pltpu.VMEM((256, BLOCK), BF), pltpu.VMEM((169, BLOCK), BF),
            pltpu.VMEM((256, 256), F32), pltpu.VMEM((176, 256), F32),
        ],
        compiler_params=PARAMS,
    )(
        edge_count, nodes, low, high, w_qkv, gains, source, target, rows, part, edges,
        core, head_in, head_out.T, targets,
    )
    chips = ("pair", "gx", "gy")
    other = swap_cores(send)
    nodes = pl.pallas_call(update_kernel, out_shape=square, compiler_params=SMALL, cost_estimate=cost(1))(nodes, acc, gains)
    other, nodes = lax.optimization_barrier((other, nodes))
    parts = lax.all_to_all(keep + other, chips, 0, 0, tiled=True)
    share = jnp.sum(parts, axis=0)
    full = lax.all_to_all(jnp.broadcast_to(share[None], (128, 8, 128)), AXES, 0, 0, tiled=True)
    full = full.reshape(2, 2, 32, 8, 128)
    grad_in = full[:, 0].reshape(64, 8, 128)
    grad_out = full[:, 1].reshape(64, 8, 128)[0:44]
    grad_in = grad_in.reshape(32, 2, 8, 128).transpose(0, 2, 1, 3).reshape(256, 256)
    grad_out = grad_out.reshape(22, 2, 8, 128).transpose(0, 2, 1, 3).reshape(176, 256)[0:169].T
    return nodes, grad_in, grad_out


def solution(mesh):
    shape = dict(mesh.shape)
    cut = Mesh(mesh.devices.reshape(shape["rep"] // 2, 2, shape["gx"], shape["gy"]), AXES)
    tile = P(AXES)
    return jax.shard_map(
        body,
        mesh=cut,
        in_specs=(
            P(AXES, None), P(AXES, None), tile, tile, tile, P(("pair", "core"), "gx", "gy", None, None, None),
            P(), P(), P(), P(), P(), P(None, AXES),
        ),
        out_specs=(P(AXES, None), P(), P()),
        check_vma=False,
    )
```
